256 devices in a mesh: fsdp: 64 (over z, y, core), rep: 4 (over x).
Axes of the slice: x: 4, y: 4, z: 8, core: 2. Of those that a mesh axis runs over, the one named last changes fastest.
Arguments:
- grads: float32 [64, 4, 192, 768], P(None, 'rep', 'fsdp'), may hold values from -9 to 9
- params: bfloat16 [64, 4, 192, 768], P(None, 'rep', 'fsdp'), may hold values from -3 to 3
- owner_slot: int32 [64], replicated, may hold values from 0 to 127, as said below
- left_stats: float32 [128, 768, 768], P('fsdp', 'rep'), may hold values from -0.1 to 1, as said below
- right_stats: float32 [128, 768, 768], P('fsdp', 'rep'), may hold values from -0.1 to 1, as said below
- left_root: float32 [128, 768, 768], P('fsdp', 'rep'), may hold values from -0.3 to 2, as said below
- right_root: float32 [128, 768, 768], P('fsdp', 'rep'), may hold values from -0.3 to 2, as said below
Outputs:
- new_params: bfloat16 [64, 4, 192, 768], P(None, 'rep', 'fsdp')
- update: float32 [64, 4, 192, 768], P(None, 'rep', 'fsdp')
- new_left_stats: float32 [128, 768, 768], P('fsdp', 'rep')
- new_right_stats: float32 [128, 768, 768], P('fsdp', 'rep')
The draws below stay inside these ranges and needn't reach their ends.
Inputs may be any that keep to these rules, and one draw needn't show every extreme that they name: `owner_slot`: the 64 entries are distinct; slot s belongs to the device s // 2 of fsdp; in every draw some device of fsdp holds 2 blocks. `left_stats`: each slot's matrix is symmetric. `right_stats`: each slot's matrix is symmetric. `left_root`: each slot's matrix is symmetric. `right_root`: each slot's matrix is symmetric.
All inputs are finite; a program needn't handle non-finite values.
Results may differ from the reference program's by a relative error of at most 0.001.
Values sent between devices are 32-bit elements; how exact they have to be, the bound alone decides.
A program may use at most 64 MiB of HBM per device.

```python
import math
import jax
import jax.numpy as jnp
from jax import lax

BLOCK = 768
BLOCKS = 64
ALL_SLOTS = 128
STRIPE = 192
N_REP = 4


def symmetric_draw(key, diagonal, spread):
    entries = jnp.clip(jax.random.normal(key, (ALL_SLOTS, BLOCK, BLOCK), jnp.float32), -5.0, 5.0)
    offdiag = (entries + jnp.swapaxes(entries, 1, 2)) * (spread / math.sqrt(BLOCK))
    identity = jnp.eye(BLOCK, dtype=jnp.float32)
    return offdiag * (1.0 - identity) + identity * diagonal[:, :, None]


def draw_grads(key, part):
    key = jax.random.fold_in(key, 11)
    first, second, third = jax.random.split(key, 3)
    positions = jnp.arange(BLOCK).astype(jnp.float32)
    rising = jnp.exp(math.log(3.0) * positions / (BLOCK - 1))
    row_scale = rising[None, :] * jnp.exp(jax.random.uniform(first, (BLOCKS, BLOCK), jnp.float32, math.log(0.5), math.log(2.0)))
    col_scale = jnp.exp(jax.random.uniform(second, (BLOCKS, BLOCK), jnp.float32, math.log(0.3), math.log(3.0)))
    noise = jnp.clip(jax.random.normal(third, (BLOCKS, BLOCK, BLOCK), jnp.float32), -5.0, 5.0)
    values = 0.1 * noise * row_scale[:, :, None] * col_scale[:, None, :]
    return values.reshape(BLOCKS, BLOCK // STRIPE, STRIPE, BLOCK)


def draw_owner_slot(key, part):
    key = jax.random.fold_in(key, 5)
    shuffled = jax.random.permutation(key, ALL_SLOTS).astype(jnp.int32)
    leading = shuffled[:BLOCKS]
    partner = leading[0] + 1 - 2 * (leading[0] % 2)
    present = jnp.any(leading == partner)
    second = jnp.where(present, leading[1], partner)
    return leading.at[1].set(second)


def draw_left_stats(key, part):
    key = jax.random.fold_in(key, 21)
    first, second = jax.random.split(key)
    diagonal = jnp.exp(jax.random.uniform(first, (ALL_SLOTS, BLOCK), jnp.float32, math.log(0.2), math.log(1.0)))
    return symmetric_draw(second, diagonal, 0.05)


def draw_right_stats(key, part):
    key = jax.random.fold_in(key, 22)
    first, second = jax.random.split(key)
    diagonal = jnp.exp(jax.random.uniform(first, (ALL_SLOTS, BLOCK), jnp.float32, math.log(0.2), math.log(1.0)))
    return symmetric_draw(second, diagonal, 0.05)


def draw_left_root(key, part):
    key = jax.random.fold_in(key, 31)
    first, second = jax.random.split(key)
    diagonal = jnp.exp(jax.random.uniform(first, (ALL_SLOTS, BLOCK), jnp.float32, math.log(0.5), math.log(2.0)))
    return symmetric_draw(second, diagonal, 0.3)


def draw_right_root(key, part):
    key = jax.random.fold_in(key, 32)
    first, second = jax.random.split(key)
    diagonal = jnp.exp(jax.random.uniform(first, (ALL_SLOTS, BLOCK), jnp.float32, math.log(0.5), math.log(2.0)))
    return symmetric_draw(second, diagonal, 0.3)


def levels(own_key, dims, shards, low, top_value):
    loudness = 1.0
    for dim, blocks in shards:
        steps = jax.random.uniform(jax.random.fold_in(jax.random.fold_in(own_key, 6), dim), (blocks,), jnp.float32, low / len(shards), top_value / len(shards))
        loudness = loudness * jnp.repeat(jnp.exp(steps), dims[dim] // blocks).reshape((-1,) + (1,) * (len(dims) - 1 - dim))
    return loudness


def scatter_about(rng, dims, scale, most, shards=(), held_as=jnp.bfloat16):
    drawn = jax.random.normal(rng, dims, jnp.float32) * scale
    if len(shards) > 0:
        drawn = levels(rng, dims, shards, -0.22, 0.18) * drawn
    return jnp.clip(drawn, min=-most, max=most).astype(held_as)


def setup_inputs(seed: int = 0) -> dict:
    seeds = jax.random.split(jax.random.key(seed), 8)
    grads = draw_grads(jax.random.fold_in(seeds[7], 71), 0)
    params = scatter_about(seeds[1], (BLOCKS, N_REP, STRIPE, BLOCK), 0.5, 3.0, ((1, 4), (2, 64)))
    owner_slot = draw_owner_slot(jax.random.fold_in(seeds[7], 71), 0)
    left_stats = draw_left_stats(jax.random.fold_in(seeds[7], 71), 0)
    right_stats = draw_right_stats(jax.random.fold_in(seeds[7], 71), 0)
    left_root = draw_left_root(jax.random.fold_in(seeds[7], 71), 0)
    right_root = draw_right_root(jax.random.fold_in(seeds[7], 71), 0)
    return {"grads": grads, "params": params, "owner_slot": owner_slot, "left_stats": left_stats, "right_stats": right_stats, "left_root": left_root, "right_root": right_root}


STAT_DECAY = 0.95
STEP_SIZE = 0.25
EPSILON = 1e-06
HIGHEST_PREC = lax.Precision.HIGHEST

def per_slot(operands):
    gradient, left_stat, right_stat, left_factor, right_factor = operands
    left_gram = jnp.dot(gradient, gradient.T, precision=HIGHEST_PREC, preferred_element_type=jnp.float32)
    right_gram = jnp.dot(gradient.T, gradient, precision=HIGHEST_PREC, preferred_element_type=jnp.float32)
    new_left = STAT_DECAY * left_stat + (1.0 - STAT_DECAY) * left_gram
    new_right = STAT_DECAY * right_stat + (1.0 - STAT_DECAY) * right_gram
    left_mixed = jnp.dot(left_factor, gradient, precision=HIGHEST_PREC, preferred_element_type=jnp.float32)
    precond = jnp.dot(left_mixed, right_factor, precision=HIGHEST_PREC, preferred_element_type=jnp.float32)
    grad_mean = jnp.mean(gradient * gradient)
    prec_mean = jnp.mean(precond * precond)
    grafted = precond * jnp.sqrt(grad_mean / (prec_mean + EPSILON))
    return (new_left, new_right, grafted)

def reference(grads, params, owner_slot, left_stats, right_stats, left_root, right_root):
    blocks_full = grads.reshape(BLOCKS, BLOCK, BLOCK)
    slotted = jnp.zeros((ALL_SLOTS, BLOCK, BLOCK), jnp.float32).at[owner_slot].set(blocks_full)
    new_left, new_right, grafted = lax.map(per_slot, (slotted, left_stats, right_stats, left_root, right_root))
    update = grafted[owner_slot].reshape(grads.shape)
    new_params = (params.astype(jnp.float32) - STEP_SIZE * update).astype(jnp.bfloat16)
    return (new_params, update, new_left, new_right)
```

```python
import functools

import jax
import jax.numpy as jnp
from jax import lax
from jax.experimental import pallas as pl
from jax.experimental.pallas import tpu as pltpu
from jax.sharding import PartitionSpec as P

STAT_DECAY = 0.95
STEP_SIZE = 0.25
EPSILON = 1e-06
LANES = 128
F32 = jnp.float32
BF16 = jnp.bfloat16
NN = (((1,), (0,)), ((), ()))
NT = (((1,), (1,)), ((), ()))


def split(value):
    high = value.astype(BF16)
    return high, (value - high.astype(F32)).astype(BF16)


def dot3(left, right, dims):
    dot = functools.partial(lax.dot_general, dimension_numbers=dims, preferred_element_type=F32)
    return dot(left[0], right[0]) + (dot(left[0], right[1]) + dot(left[1], right[0]))


def kernel(
    nf, nx, rows, groups, blocks,
    slot_block, owner, grads, params, left_root, right_root, left_stats, right_stats,
    update, new_params, new_left, new_right,
    grads_v, send, gath, back, ret, upd_t, left_v, lstat_v, rstat_v,
    root_f, root_h, root_l, gh, gl, gt, lh, ll, lgh, lgl, prec, sq,
    in_sem, out_sem, a_send, a_recv, r_send, r_recv, x_send, x_recv, f_send, f_recv,
    s_send, s_recv, u_send, u_recv,
):
    slots, stripe, width = left_v.shape
    panels = width // LANES
    half = width // 2
    packet = rows * panels
    size = nf // groups
    chunk = size * rows
    me = lax.axis_index("fsdp")
    x = lax.axis_index("rep")
    mz, mg = me // size, me % size
    right_x, left_x, far_x = (x + 1) % nx, (x + nx - 1) % nx, (x + 2) % nx
    h, pos = x // 2, x % 2
    mate = h * 2 + 1 - pos
    other = jnp.where(pos == 0, left_x, right_x)

    def at_x(target):
        return {"fsdp": me, "rep": target}

    def at_f(target):
        return {"fsdp": target, "rep": x}

    def remote(src, dst, send_sem, recv_sem, device):
        return pltpu.make_async_remote_copy(
            src_ref=src, dst_ref=dst, send_sem=send_sem, recv_sem=recv_sem,
            device_id=device, device_id_type=pl.DeviceIdType.MESH,
        )

    def await_bytes(ref, sem):
        pltpu.make_async_copy(ref, ref, sem).wait()

    order = [0]
    for step in range(groups // 2, 0, -1):
        order.append(step)
        if step != groups - step:
            order.append(groups - step)

    load_grads = pltpu.make_async_copy(grads, grads_v.at[pl.ds(0, blocks * packet)], in_sem.at[0])
    load_grads.start()
    load_left = pltpu.make_async_copy(left_root, left_v, in_sem.at[1])
    load_left.start()
    loads_r = []
    for t in range(slots):
        for kind in range(2):
            col = h if kind == 0 else 1 - h
            cols = pl.ds(pl.multiple_of(col * half, LANES), half)
            src = right_root.at[t, :, cols]
            load = pltpu.make_async_copy(
                src, root_f.at[t, kind, pl.ds(pl.multiple_of(pos * stripe, 8), stripe)], in_sem.at[2 + 2 * t + kind]
            )
            load.start()
            loads_r.append(load)
    load_ls = pltpu.make_async_copy(left_stats, lstat_v, in_sem.at[6])
    load_ls.start()
    load_rs = pltpu.make_async_copy(right_stats, rstat_v, in_sem.at[7])
    load_rs.start()

    barrier = pltpu.get_barrier_semaphore()

    def greet(k, carry):
        pl.semaphore_signal(barrier, inc=1, device_id=at_f((me + k) % nf), device_id_type=pl.DeviceIdType.MESH)
        return carry

    lax.fori_loop(1, nf, greet, 0)
    for d in range(1, nx):
        pl.semaphore_signal(barrier, inc=1, device_id=at_x((x + d) % nx), device_id_type=pl.DeviceIdType.MESH)
    pl.semaphore_wait(barrier, nf - 1 + nx - 1)

    root_sends = []
    root_fwds = []
    for t in range(slots):
        for kind in range(2):
            loads_r[2 * t + kind].wait()
        my_rows = pl.ds(pl.multiple_of(pos * stripe, 8), stripe)
        mate_rows = pl.ds(pl.multiple_of((1 - pos) * stripe, 8), stripe)
        group = [
            remote(root_f.at[t, 0, my_rows], root_f.at[t, 2, my_rows], r_send.at[t, 2], r_recv.at[t, 2], at_x(other)),
            remote(root_f.at[t, 0, my_rows], root_f.at[t, 0, my_rows], r_send.at[t, 0], r_recv.at[t, 0], at_x(mate)),
            remote(root_f.at[t, 1, my_rows], root_f.at[t, 1, my_rows], r_send.at[t, 1], r_recv.at[t, 1], at_x(mate)),
        ]
        for copy in group:
            copy.start()
        root_sends += group
        root_fwds.append(
            remote(root_f.at[t, 0, mate_rows], root_f.at[t, 2, mate_rows], r_send.at[t, 3], r_recv.at[t, 3], at_x(other))
        )

    load_grads.wait()
    flat_grads = grads_v.reshape((blocks + 1) * packet, LANES)
    flat_grads[pl.ds(blocks * packet, packet), :] = jnp.zeros((packet, LANES), F32)
    flat_send = send.reshape(slots * nf * packet, LANES)

    def pack(t, dest):
        block = slot_block[slots * dest + t]
        for j in range(rows):
            value = flat_grads[pl.ds(block * packet + panels * j, panels), :]
            flat_send[pl.ds((t * nf + dest) * packet + j, panels, stride=rows), :] = value

    for t in range(slots):
        mine = gath.at[t, x, :, pl.ds(me * rows, rows)]
        pack(t, me)
        pltpu.make_async_copy(send.at[t, me], mine, a_recv.at[t, mz]).start()
        for offset in order:
            dz = (mz + offset) % groups

            def post(k, carry, t=t, dz=dz, mine=mine):
                dest = dz * size + (mg + k) % size
                pack(t, dest)
                remote(send.at[t, dest], mine, a_send.at[t], a_recv.at[t, mz], at_f(dest)).start()
                return carry

            lax.fori_loop(1 if offset == 0 else 0, size, post, 0)

    load_left.wait()
    for t in range(slots):
        lh[t], ll[t] = split(left_v[t])

    def rows_of(k):
        source = (mz + groups - order[k]) % groups
        return source, pl.ds(source * chunk, chunk)

    def direct(t, k, side):
        source, part = rows_of(k)
        ref = gath.at[t, x, :, part]
        return remote(ref, ref, x_send.at[t, side, k], x_recv.at[t, side, k], at_x(right_x if side == 0 else left_x))

    def arrival(t, k, side):
        source, part = rows_of(k)
        ref = gath.at[t, left_x if side == 0 else right_x, :, part]
        return remote(ref, ref, x_send.at[t, side, k], x_recv.at[t, side, k], at_x(right_x if side == 0 else left_x))

    def forward(t, k):
        source, part = rows_of(k)
        side = k % 2
        ref = gath.at[t, left_x if side == 0 else right_x, :, part]
        return remote(ref, ref, f_send.at[t, k], f_recv.at[t, k], at_x(right_x if side == 0 else left_x))

    def far_arrival(t, k):
        source, part = rows_of(k)
        ref = gath.at[t, far_x, :, part]
        return remote(ref, ref, f_send.at[t, k], f_recv.at[t, k], at_x(right_x))

    def spread(t):
        for k in range(groups):
            source, part = rows_of(k)
            await_bytes(gath.at[t, x, :, part], a_recv.at[t, source])
            direct(t, k, 0).start()
            direct(t, k, 1).start()

    def relay(t):
        for k in range(groups):
            side = k % 2
            arrival(t, k, side).wait_recv()
            forward(t, k).start()

    g4 = gath.reshape(slots, nx, panels, stripe, LANES)
    ret4 = ret.reshape(slots, panels, stripe, LANES)

    def take(t, i):
        total = jnp.zeros((1, LANES), F32)
        part = pl.ds(pl.multiple_of(i * stripe, 16), stripe)
        for c in range(panels):
            value = g4[t, i, c]
            total = total + jnp.sum(value * value, axis=0, keepdims=True)
            high, low = split(value)
            gh[t, part, c * LANES : (c + 1) * LANES] = high
            gl[t, part, c * LANES : (c + 1) * LANES] = low
        return total

    def take_root(t):
        for kind in range(3):
            root_h[t, kind], root_l[t, kind] = split(root_f[t, kind])

    def precondition(t):
        for c in range(2):
            cols = slice(c * half, (c + 1) * half)
            mixed = dot3((lh[t], ll[t]), (gh[t, :, cols], gl[t, :, cols]), NN)
            lgh[c], lgl[c] = split(mixed)
        near = (lgh[h], lgl[h])
        away = (lgh[1 - h], lgl[1 - h])
        root = [(root_h[t, kind], root_l[t, kind]) for kind in range(3)]
        prec_near = dot3(near, root[0], NN) + dot3(away, root[1], NT)
        prec_away = dot3(near, root[1], NN) + dot3(away, root[2], NN)
        squares = jnp.sum(prec_near * prec_near + prec_away * prec_away, axis=0, keepdims=True)
        per = half // LANES
        for c in range(per):
            cols = slice(c * LANES, (c + 1) * LANES)
            prec[h * per + c] = prec_near[:, cols]
            prec[(1 - h) * per + c] = prec_away[:, cols]
        sq[t, x] = jnp.broadcast_to(jnp.sum(squares, axis=1, keepdims=True), sq.shape[2:])
        for d in range(1, nx):
            remote(sq.at[t, x], sq.at[t, x], s_send.at[t, d - 1], s_recv.at[t, d - 1], at_x((x + d) % nx)).start()

    def square_wait(t):
        for d in range(1, nx):
            source = (x + nx - d) % nx
            remote(sq.at[t, source], sq.at[t, source], s_send.at[t, d - 1], s_recv.at[t, d - 1], at_x((x + d) % nx)).wait_recv()

    def give_back(t, grad_squares):
        prec_mean = (((sq[t, 0] + sq[t, 1]) + sq[t, 2]) + sq[t, 3]) / (width * width)
        grad_mean = jnp.sum(grad_squares, axis=1, keepdims=True) / (width * width)
        scale = jnp.sqrt(grad_mean / (prec_mean[0:1, :] + EPSILON))
        for c in range(panels):
            ret4[t, c] = prec[c] * scale
        own = ret.at[t, :, pl.ds(me * rows, rows)]
        pltpu.make_async_copy(own, back.at[t, me], u_recv.at[t]).start()
        for offset in order:
            dz = (mz + offset) % groups

            def post(k, carry, dz=dz):
                dest = dz * size + (mg + k) % size
                remote(
                    ret.at[t, :, pl.ds(dest * rows, rows)], back.at[t, me], u_send.at[t], u_recv.at[t], at_f(dest)
                ).start()
                return carry

            lax.fori_loop(1 if offset == 0 else 0, size, post, 0)

    def left_gram(t):
        mine = pl.ds(pl.multiple_of(x * stripe, 16), stripe)
        ours = (gh[t, mine], gl[t, mine])
        for n in range(3):
            part = slice(n * 256, (n + 1) * 256)
            gram = dot3(ours, (gh[t, part], gl[t, part]), NT)
            lstat_v[t, :, part] = STAT_DECAY * lstat_v[t, :, part] + (1.0 - STAT_DECAY) * gram
        pltpu.make_async_copy(lstat_v.at[t], new_left.at[t], out_sem.at[t]).start()

    def right_gram(t):
        first = (3 * x) // 2
        for i in range(nx):
            pair = jnp.concatenate([g4[t, i, first], g4[t, i, first + 1]], axis=1)
            gt[:, i * stripe : (i + 1) * stripe] = pair.T
        ours = split(gt[pl.ds(pl.multiple_of(pos * (LANES // 2), 8), stripe), :])
        for n in range(3):
            part = slice(n * 256, (n + 1) * 256)
            gram = dot3(ours, (gh[t, :, part], gl[t, :, part]), NN)
            rstat_v[t, :, part] = STAT_DECAY * rstat_v[t, :, part] + (1.0 - STAT_DECAY) * gram
        pltpu.make_async_copy(rstat_v.at[t], new_right.at[t], out_sem.at[2 + t]).start()

    def root_relay(t):
        remote(
            root_f.at[t, 0, mate_rows], root_f.at[t, 0, mate_rows], r_send.at[t, 0], r_recv.at[t, 0], at_x(mate)
        ).wait_recv()
        root_fwds[t].start()

    def root_finish(t):
        remote(
            root_f.at[t, 1, mate_rows], root_f.at[t, 1, mate_rows], r_send.at[t, 1], r_recv.at[t, 1], at_x(mate)
        ).wait_recv()
        remote(
            root_f.at[t, 2, mate_rows], root_f.at[t, 2, mate_rows], r_send.at[t, 2], r_recv.at[t, 2], at_x(other)
        ).wait_recv()
        remote(
            root_f.at[t, 2, my_rows], root_f.at[t, 2, my_rows], r_send.at[t, 3], r_recv.at[t, 3], at_x(other)
        ).wait_recv()

    def gather_rest(t, sides):
        for k in range(groups):
            if k % 2 != sides:
                continue
            arrival(t, k, 1 - sides).wait_recv()

    totals = [None] * slots
    root_relay(0)
    spread(0)
    root_relay(1)
    relay(0)
    spread(1)
    root_finish(0)
    take_root(0)
    for t in range(slots):
        totals[t] = take(t, x)
        gather_rest(t, 0)
        gather_rest(t, 1)
        totals[t] = totals[t] + take(t, left_x) + take(t, right_x)
        for k in range(groups):
            far_arrival(t, k).wait_recv()
        totals[t] = totals[t] + take(t, far_x)
        precondition(t)
        if t == 0:
            load_ls.wait()
            load_rs.wait()
            relay(1)
            square_wait(0)
            give_back(0, totals[0])
            left_gram(0)
            root_finish(1)
            take_root(1)
        else:
            square_wait(1)
            give_back(1, totals[1])
            right_gram(0)
            left_gram(1)
            right_gram(1)

    flat_back = back.reshape(slots * nf * packet, LANES)
    for t in range(slots):
        await_bytes(back.at[t], u_recv.at[t])

    def place(b, carry):
        slot = owner[b]
        start = ((slot % slots) * nf + slot // slots) * packet
        for c in range(panels):
            value = flat_back[pl.ds(start + rows * c, rows), :]
            update[pl.ds(b * packet + c, rows, stride=panels), :] = value
            upd_t[pl.ds(c * blocks + b, rows, stride=panels * blocks), :] = value
        return carry

    lax.fori_loop(0, blocks, place, 0)
    for j in range(rows):
        for c in range(panels):
            cols = slice(c * LANES, (c + 1) * LANES)
            step = STEP_SIZE * upd_t[(j * panels + c) * blocks : (j * panels + c + 1) * blocks, :]
            new_params[j, :, cols] = (params[j, :, cols].astype(F32) - step).astype(BF16)

    for t in range(slots):
        pltpu.make_async_copy(lstat_v.at[t], new_left.at[t], out_sem.at[t]).wait()
        pltpu.make_async_copy(rstat_v.at[t], new_right.at[t], out_sem.at[2 + t]).wait()
        await_bytes(send.at[t, pl.ds(0, nf - 1)], a_send.at[t])
        await_bytes(back.at[t, pl.ds(0, nf - 1)], u_send.at[t])
        for k in range(groups):
            direct(t, k, 0).wait_send()
            direct(t, k, 1).wait_send()
            forward(t, k).wait_send()
        for d in range(1, nx):
            remote(sq.at[t, x], sq.at[t, x], s_send.at[t, d - 1], s_recv.at[t, d - 1], at_x((x + d) % nx)).wait_send()
    for copy in root_sends:
        copy.wait_send()
    for copy in root_fwds:
        copy.wait_send()


def on_device(grads, params, owner_slot, left_stats, right_stats, left_root, right_root):
    blocks, _, rows, width = grads.shape
    nf = lax.axis_size("fsdp")
    nx = lax.axis_size("rep")
    slots, stripe, _ = left_stats.shape
    panels = width // LANES
    half = width // 2
    packet = rows * panels
    groups = 8 if nf >= 64 else 2
    slot_ids = jnp.arange(slots * nf, dtype=jnp.int32)
    block_ids = jnp.arange(blocks, dtype=jnp.int32)
    slot_block = jnp.min(
        jnp.where(owner_slot[None, :] == slot_ids[:, None], block_ids[None, :], blocks), axis=1
    )
    flat = grads.reshape(blocks * packet, 1, LANES)
    params_t = params.reshape(blocks, rows, width).transpose(1, 0, 2)
    hbm = pl.BlockSpec(memory_space=pl.ANY)
    vmem = pl.BlockSpec(memory_space=pltpu.VMEM)
    smem = pl.BlockSpec(memory_space=pltpu.SMEM)
    dma = pltpu.SemaphoreType.DMA
    update, new_params, new_left, new_right = pl.pallas_call(
        functools.partial(kernel, nf, nx, rows, groups, blocks),
        out_shape=(
            jax.ShapeDtypeStruct((blocks * packet, LANES), F32),
            jax.ShapeDtypeStruct((rows, blocks, width), BF16),
            jax.ShapeDtypeStruct(left_stats.shape, F32),
            jax.ShapeDtypeStruct(right_stats.shape, F32),
        ),
        in_specs=[smem, smem, hbm, vmem, hbm, hbm, hbm, hbm],
        out_specs=(vmem, vmem, hbm, hbm),
        scratch_shapes=[
            pltpu.VMEM(((blocks + 1) * packet, 1, LANES), F32),
            pltpu.VMEM((slots, nf, panels, rows, 1, LANES), F32),
            pltpu.VMEM((slots, nx, panels, stripe, 1, LANES), F32),
            pltpu.VMEM((slots, nf, panels, rows, 1, LANES), F32),
            pltpu.VMEM((slots, panels, stripe, 1, LANES), F32),
            pltpu.VMEM((blocks * packet, LANES), F32),
            pltpu.VMEM((slots, stripe, width), F32),
            pltpu.VMEM((slots, stripe, width), F32),
            pltpu.VMEM((slots, stripe, width), F32),
            pltpu.VMEM((slots, 3, half, half), F32),
            pltpu.VMEM((slots, 3, half, half), BF16),
            pltpu.VMEM((slots, 3, half, half), BF16),
            pltpu.VMEM((slots, width, width), BF16),
            pltpu.VMEM((slots, width, width), BF16),
            pltpu.VMEM((2 * LANES, width), F32),
            pltpu.VMEM((slots, stripe, width), BF16),
            pltpu.VMEM((slots, stripe, width), BF16),
            pltpu.VMEM((2, stripe, half), BF16),
            pltpu.VMEM((2, stripe, half), BF16),
            pltpu.VMEM((panels, stripe, LANES), F32),
            pltpu.VMEM((slots, nx, 8, LANES), F32),
            dma((8,)),
            dma((4,)),
            dma((slots,)),
            dma((slots, groups)),
            dma((slots, 4)),
            dma((slots, 4)),
            dma((slots, 2, groups)),
            dma((slots, 2, groups)),
            dma((slots, groups)),
            dma((slots, groups)),
            dma((slots, nx - 1)),
            dma((slots, nx - 1)),
            dma((slots,)),
            dma((slots,)),
        ],
        compiler_params=pltpu.CompilerParams(
            collective_id=0, has_side_effects=True, vmem_limit_bytes=56 * 1024 * 1024
        ),
    )(slot_block, owner_slot, flat, params_t, left_root, right_root, left_stats, right_stats)
    update = update.reshape(blocks, 1, rows, width)
    new_params = new_params.transpose(1, 0, 2).reshape(blocks, 1, rows, width)
    return (new_params, update, new_left, new_right)


def solution(mesh):
    in_specs = (
        P(None, "rep", "fsdp", None),
        P(None, "rep", "fsdp", None),
        P(),
        P("fsdp", "rep", None),
        P("fsdp", "rep", None),
        P("fsdp", "rep", None),
        P("fsdp", "rep", None),
    )
    out_specs = (
        P(None, "rep", "fsdp", None),
        P(None, "rep", "fsdp", None),
        P("fsdp", "rep", None),
        P("fsdp", "rep", None),
    )
    return jax.shard_map(
        on_device, mesh=mesh, in_specs=in_specs, out_specs=out_specs, check_vma=False
    )
```

```python
import functools

import jax
import jax.numpy as jnp
from jax import lax
from jax.experimental import pallas as pl
from jax.experimental.pallas import tpu as pltpu
from jax.sharding import PartitionSpec as P

STAT_DECAY = 0.95
STEP_SIZE = 0.25
EPSILON = 1e-06
LANES = 128
F32 = jnp.float32
BF16 = jnp.bfloat16
NN = (((1,), (0,)), ((), ()))
NT = (((1,), (1,)), ((), ()))


def split(value):
    high = value.astype(BF16)
    return high, (value - high.astype(F32)).astype(BF16)


def dot3(left, right, dims):
    dot = functools.partial(lax.dot_general, dimension_numbers=dims, preferred_element_type=F32)
    return dot(left[0], right[0]) + (dot(left[0], right[1]) + dot(left[1], right[0]))


def kernel(
    nf, nx, rows, groups, blocks,
    owner, grads, left_root, right_root, left_stats, right_stats,
    back, new_left, new_right,
    blocks_v, slot_block, grads_v, send, gath, ret, left_v, lstat_v, rstat_v,
    root_f, root_h, root_l, gh, gl, gt, lh, ll, lgh, lgl, prec, sq,
    in_sem, out_sem, a_send, a_recv, r_send, r_recv, x_send, x_recv, f_send, f_recv,
    s_send, s_recv, u_send, u_recv, turned,
):
    slots, stripe, width = left_v.shape
    panels = width // LANES
    half = width // 2
    packet = rows * panels
    size = nf // groups
    chunk = size * rows
    me = lax.axis_index("fsdp")
    x = lax.axis_index("rep")
    mz, mg = me // size, me % size
    right_x, left_x, far_x = (x + 1) % nx, (x + nx - 1) % nx, (x + 2) % nx
    h, pos = x // 2, x % 2
    mate = h * 2 + 1 - pos
    other = jnp.where(pos == 0, left_x, right_x)

    def at_x(target):
        return {"fsdp": me, "rep": target}

    def at_f(target):
        return {"fsdp": target, "rep": x}

    def remote(src, dst, send_sem, recv_sem, device):
        return pltpu.make_async_remote_copy(
            src_ref=src, dst_ref=dst, send_sem=send_sem, recv_sem=recv_sem,
            device_id=device, device_id_type=pl.DeviceIdType.MESH,
        )

    def await_bytes(ref, sem):
        pltpu.make_async_copy(ref, ref, sem).wait()

    order = [0]
    for step in range(groups // 2, 0, -1):
        order.append(step)
        if step != groups - step:
            order.append(groups - step)

    load_grads = pltpu.make_async_copy(grads, grads_v.at[pl.ds(0, blocks * packet)], in_sem.at[0])
    load_grads.start()
    load_left = pltpu.make_async_copy(left_root, left_v, in_sem.at[1])
    load_left.start()
    loads_r = []
    for t in range(slots):
        for kind in range(2):
            col = h if kind == 0 else 1 - h
            cols = pl.ds(pl.multiple_of(col * half, LANES), half)
            src = right_root.at[t, :, cols]
            load = pltpu.make_async_copy(
                src, root_f.at[t, kind, pl.ds(pl.multiple_of(pos * stripe, 8), stripe)], in_sem.at[2 + 2 * t + kind]
            )
            load.start()
            loads_r.append(load)
    load_ls = pltpu.make_async_copy(left_stats, lstat_v, in_sem.at[6])
    load_ls.start()
    load_rs = pltpu.make_async_copy(right_stats, rstat_v, in_sem.at[7])
    load_rs.start()

    barrier = pltpu.get_barrier_semaphore()

    def greet(k, carry):
        pl.semaphore_signal(barrier, inc=1, device_id=at_f((me + k) % nf), device_id_type=pl.DeviceIdType.MESH)
        return carry

    lax.fori_loop(1, nf, greet, 0)
    for d in range(1, nx):
        pl.semaphore_signal(barrier, inc=1, device_id=at_x((x + d) % nx), device_id_type=pl.DeviceIdType.MESH)

    row = jnp.broadcast_to(owner[...], (blocks, blocks))
    down = lax.broadcasted_iota(jnp.int32, (blocks, blocks), 0)
    along = lax.broadcasted_iota(jnp.int32, (blocks, blocks), 1)
    column = jnp.sum(jnp.where(down == along, row, 0), axis=1, keepdims=True)
    slot_ids = lax.broadcasted_iota(jnp.int32, (blocks, slots * nf), 1)
    block_ids = lax.broadcasted_iota(jnp.int32, (blocks, slots * nf), 0)
    held = blocks + jnp.sum(jnp.where(column == slot_ids, block_ids - blocks, 0), axis=0, keepdims=True)
    blocks_v[...] = jnp.maximum(held, 0)
    to_smem = pltpu.make_async_copy(blocks_v, slot_block, in_sem.at[8])
    to_smem.start()
    pl.semaphore_wait(barrier, nf - 1 + nx - 1)

    def diag(t, kind, q):
        return root_f.at[t, kind, pl.ds(pl.multiple_of(q * stripe, 8), stripe), pl.ds(pl.multiple_of(q * LANES, LANES), 2 * LANES)]

    root_sends = []
    root_fwds = []
    for t in range(slots):
        for kind in range(2):
            loads_r[2 * t + kind].wait()
        my_rows = pl.ds(pl.multiple_of(pos * stripe, 8), stripe)
        mate_rows = pl.ds(pl.multiple_of((1 - pos) * stripe, 8), stripe)
        group = [
            remote(root_f.at[t, 0, my_rows], root_f.at[t, 2, my_rows], r_send.at[t, 2], r_recv.at[t, 2], at_x(other)),
            remote(diag(t, 0, pos), diag(t, 0, pos), r_send.at[t, 0], r_recv.at[t, 0], at_x(mate)),
            remote(root_f.at[t, 1, my_rows], root_f.at[t, 1, my_rows], r_send.at[t, 1], r_recv.at[t, 1], at_x(mate)),
        ]
        for copy in group:
            copy.start()
        root_sends += group
        root_fwds.append(
            remote(diag(t, 0, 1 - pos), diag(t, 2, 1 - pos), r_send.at[t, 3], r_recv.at[t, 3], at_x(other))
        )

    load_grads.wait()
    to_smem.wait()
    flat_grads = grads_v.reshape((blocks + 1) * packet, LANES)
    flat_grads[pl.ds(blocks * packet, packet), :] = jnp.zeros((packet, LANES), F32)
    flat_send = send.reshape(slots * nf * packet, LANES)

    def pack(t, dest):
        block = slot_block[0, slots * dest + t]
        for j in range(rows):
            value = flat_grads[pl.ds(block * packet + panels * j, panels), :]
            flat_send[pl.ds((t * nf + dest) * packet + j, panels, stride=rows), :] = value

    for t in range(slots):
        mine = gath.at[t, x, :, pl.ds(me * rows, rows)]
        pack(t, me)
        pltpu.make_async_copy(send.at[t, me], mine, a_recv.at[t, mz]).start()
        for offset in order:
            dz = (mz + offset) % groups

            def post(k, carry, t=t, dz=dz, mine=mine):
                dest = dz * size + (mg + k) % size
                pack(t, dest)
                remote(send.at[t, dest], mine, a_send.at[t], a_recv.at[t, mz], at_f(dest)).start()
                return carry

            lax.fori_loop(1 if offset == 0 else 0, size, post, 0)

    load_left.wait()
    for t in range(slots):
        lh[t], ll[t] = split(left_v[t])

    def rows_of(k):
        source = (mz + groups - order[k]) % groups
        return source, pl.ds(source * chunk, chunk)

    def direct(t, k, side):
        source, part = rows_of(k)
        ref = gath.at[t, x, :, part]
        return remote(ref, ref, x_send.at[t, side, k], x_recv.at[t, side, k], at_x(right_x if side == 0 else left_x))

    def arrival(t, k, side):
        source, part = rows_of(k)
        ref = gath.at[t, left_x if side == 0 else right_x, :, part]
        return remote(ref, ref, x_send.at[t, side, k], x_recv.at[t, side, k], at_x(right_x if side == 0 else left_x))

    def forward(t, k):
        source, part = rows_of(k)
        side = k % 2
        ref = gath.at[t, left_x if side == 0 else right_x, :, part]
        return remote(ref, ref, f_send.at[t, k], f_recv.at[t, k], at_x(right_x if side == 0 else left_x))

    def far_arrival(t, k):
        source, part = rows_of(k)
        ref = gath.at[t, far_x, :, part]
        return remote(ref, ref, f_send.at[t, k], f_recv.at[t, k], at_x(right_x))

    def spread(t):
        for k in range(groups):
            source, part = rows_of(k)
            await_bytes(gath.at[t, x, :, part], a_recv.at[t, source])
            direct(t, k, 0).start()
            direct(t, k, 1).start()

    def relay(t):
        for k in range(groups):
            side = k % 2
            arrival(t, k, side).wait_recv()
            forward(t, k).start()

    g4 = gath.reshape(slots, nx, panels, stripe, LANES)
    ret4 = ret.reshape(slots, panels, stripe, LANES)

    def take(t, i):
        total = jnp.zeros((1, LANES), F32)
        part = pl.ds(pl.multiple_of(i * stripe, 16), stripe)
        for c in range(panels):
            value = g4[t, i, c]
            total = total + jnp.sum(value * value, axis=0, keepdims=True)
            high, low = split(value)
            gh[t, part, c * LANES : (c + 1) * LANES] = high
            gl[t, part, c * LANES : (c + 1) * LANES] = low
        return total

    def take_root(t):
        for kind in range(3):
            root_h[t, kind], root_l[t, kind] = split(root_f[t, kind])

    def precondition(t):
        for c in range(2):
            cols = slice(c * half, (c + 1) * half)
            mixed = dot3((lh[t], ll[t]), (gh[t, :, cols], gl[t, :, cols]), NN)
            lgh[c], lgl[c] = split(mixed)
        near = (lgh[h], lgl[h])
        away = (lgh[1 - h], lgl[1 - h])
        root = [(root_h[t, kind], root_l[t, kind]) for kind in range(3)]
        prec_near = dot3(near, root[0], NN) + dot3(away, root[1], NT)
        prec_away = dot3(near, root[1], NN) + dot3(away, root[2], NN)
        squares = jnp.sum(prec_near * prec_near + prec_away * prec_away, axis=0, keepdims=True)
        per = half // LANES
        for c in range(per):
            cols = slice(c * LANES, (c + 1) * LANES)
            prec[h * per + c] = prec_near[:, cols]
            prec[(1 - h) * per + c] = prec_away[:, cols]
        sq[t, x] = jnp.broadcast_to(jnp.sum(squares, axis=1, keepdims=True), sq.shape[2:])
        for d in range(1, nx):
            remote(sq.at[t, x], sq.at[t, x], s_send.at[t, d - 1], s_recv.at[t, d - 1], at_x((x + d) % nx)).start()

    def square_wait(t):
        for d in range(1, nx):
            source = (x + nx - d) % nx
            remote(sq.at[t, source], sq.at[t, source], s_send.at[t, d - 1], s_recv.at[t, d - 1], at_x((x + d) % nx)).wait_recv()

    def give_back(t, grad_squares):
        prec_mean = (((sq[t, 0] + sq[t, 1]) + sq[t, 2]) + sq[t, 3]) / (width * width)
        grad_mean = jnp.sum(grad_squares, axis=1, keepdims=True) / (width * width)
        scale = jnp.sqrt(grad_mean / (prec_mean[0:1, :] + EPSILON))
        for c in range(panels):
            ret4[t, c] = prec[c] * scale
        own = ret.at[t, :, pl.ds(me * rows, rows)]
        pltpu.make_async_copy(own, back.at[t, me], u_recv.at[t]).start()
        for offset in order:
            dz = (mz + offset) % groups

            def post(k, carry, dz=dz):
                dest = dz * size + (mg + k) % size
                remote(
                    ret.at[t, :, pl.ds(dest * rows, rows)], back.at[t, me], u_send.at[t], u_recv.at[t], at_f(dest)
                ).start()
                return carry

            lax.fori_loop(1 if offset == 0 else 0, size, post, 0)

    def left_gram(t):
        mine = pl.ds(pl.multiple_of(x * stripe, 16), stripe)
        ours = (gh[t, mine], gl[t, mine])
        for n in range(3):
            part = slice(n * 256, (n + 1) * 256)
            gram = dot3(ours, (gh[t, part], gl[t, part]), NT)
            lstat_v[t, :, part] = STAT_DECAY * lstat_v[t, :, part] + (1.0 - STAT_DECAY) * gram
        pltpu.make_async_copy(lstat_v.at[t], new_left.at[t], out_sem.at[t]).start()

    def right_gram(t):
        first = (3 * x) // 2
        for i in range(nx):
            pair = jnp.concatenate([g4[t, i, first], g4[t, i, first + 1]], axis=1)
            gt[:, i * stripe : (i + 1) * stripe] = pair.T
        ours = split(gt[pl.ds(pl.multiple_of(pos * (LANES // 2), 8), stripe), :])
        for n in range(3):
            part = slice(n * 256, (n + 1) * 256)
            gram = dot3(ours, (gh[t, :, part], gl[t, :, part]), NN)
            rstat_v[t, :, part] = STAT_DECAY * rstat_v[t, :, part] + (1.0 - STAT_DECAY) * gram
        pltpu.make_async_copy(rstat_v.at[t], new_right.at[t], out_sem.at[2 + t]).start()

    def root_relay(t):
        remote(diag(t, 0, 1 - pos), diag(t, 0, 1 - pos), r_send.at[t, 0], r_recv.at[t, 0], at_x(mate)).wait_recv()
        root_fwds[t].start()

    def root_finish(t):
        remote(
            root_f.at[t, 1, mate_rows], root_f.at[t, 1, mate_rows], r_send.at[t, 1], r_recv.at[t, 1], at_x(mate)
        ).wait_recv()
        remote(
            root_f.at[t, 2, mate_rows], root_f.at[t, 2, mate_rows], r_send.at[t, 2], r_recv.at[t, 2], at_x(other)
        ).wait_recv()
        remote(diag(t, 2, pos), diag(t, 2, pos), r_send.at[t, 3], r_recv.at[t, 3], at_x(other)).wait_recv()
        mirror(t, 0, 1 - pos)
        mirror(t, 2, pos)

    def mirror(t, kind, q):
        panel = pl.ds(pl.multiple_of((1 - q) * 2 * LANES, LANES), LANES)
        wide = root_f[t, kind, panel, pl.ds(pl.multiple_of(q * LANES, LANES), 2 * LANES)]
        turned[...] = wide.T
        part = turned[pl.ds(pl.multiple_of(q * (LANES // 2), 8), stripe), :]
        root_f[t, kind, pl.ds(pl.multiple_of(q * stripe, 8), stripe), panel] = part

    def gather_rest(t, sides):
        for k in range(groups):
            if k % 2 != sides:
                continue
            arrival(t, k, 1 - sides).wait_recv()

    totals = [None] * slots
    root_relay(0)
    spread(0)
    root_relay(1)
    relay(0)
    spread(1)
    root_finish(0)
    take_root(0)
    for t in range(slots):
        totals[t] = take(t, x)
        gather_rest(t, 0)
        gather_rest(t, 1)
        totals[t] = totals[t] + take(t, left_x) + take(t, right_x)
        for k in range(groups):
            far_arrival(t, k).wait_recv()
        totals[t] = totals[t] + take(t, far_x)
        precondition(t)
        if t == 0:
            load_ls.wait()
            load_rs.wait()
            relay(1)
            square_wait(0)
            give_back(0, totals[0])
            left_gram(0)
            root_finish(1)
            take_root(1)
        else:
            square_wait(1)
            give_back(1, totals[1])
            right_gram(0)
            left_gram(1)
            right_gram(1)

    for t in range(slots):
        await_bytes(back.at[t], u_recv.at[t])

    for t in range(slots):
        pltpu.make_async_copy(lstat_v.at[t], new_left.at[t], out_sem.at[t]).wait()
        pltpu.make_async_copy(rstat_v.at[t], new_right.at[t], out_sem.at[2 + t]).wait()
        await_bytes(send.at[t, pl.ds(0, nf - 1)], a_send.at[t])
        await_bytes(back.at[t, pl.ds(0, nf - 1)], u_send.at[t])
        for k in range(groups):
            direct(t, k, 0).wait_send()
            direct(t, k, 1).wait_send()
            forward(t, k).wait_send()
        for d in range(1, nx):
            remote(sq.at[t, x], sq.at[t, x], s_send.at[t, d - 1], s_recv.at[t, d - 1], at_x((x + d) % nx)).wait_send()
    for copy in root_sends:
        copy.wait_send()
    for copy in root_fwds:
        copy.wait_send()


def finish(owner, back, params, left, right, update, new_params, new_left, new_right, upd_t, sem):
    copy_left = pltpu.make_async_copy(left, new_left, sem.at[0])
    copy_left.start()
    copy_right = pltpu.make_async_copy(right, new_right, sem.at[1])
    copy_right.start()
    rows, blocks, width = params.shape
    panels = width // LANES
    packet = rows * panels
    count = back.shape[0] // packet
    slots = 2
    nf = count // slots

    def place(b, carry):
        slot = owner[b]
        start = ((slot % slots) * nf + slot // slots) * packet
        for c in range(panels):
            value = back[pl.ds(start + rows * c, rows), :]
            update[pl.ds(b * packet + c, rows, stride=panels), :] = value
            upd_t[pl.ds(c * blocks + b, rows, stride=panels * blocks), :] = value
        return carry

    lax.fori_loop(0, blocks, place, 0, unroll=4)
    for j in range(rows):
        for c in range(panels):
            cols = slice(c * LANES, (c + 1) * LANES)
            step = STEP_SIZE * upd_t[(j * panels + c) * blocks : (j * panels + c + 1) * blocks, :]
            new_params[j, :, cols] = (params[j, :, cols].astype(F32) - step).astype(BF16)
    copy_left.wait()
    copy_right.wait()


def on_device(grads, params, owner_slot, left_stats, right_stats, left_root, right_root):
    blocks, _, rows, width = grads.shape
    nf = lax.axis_size("fsdp")
    nx = lax.axis_size("rep")
    slots, stripe, _ = left_stats.shape
    panels = width // LANES
    half = width // 2
    packet = rows * panels
    groups = 8 if nf >= 64 else 2
    flat = grads.reshape(blocks * packet, 1, LANES)
    params_t = params.reshape(blocks, rows, width).transpose(1, 0, 2)
    hbm = pl.BlockSpec(memory_space=pl.ANY)
    vmem = pl.BlockSpec(memory_space=pltpu.VMEM)
    smem = pl.BlockSpec(memory_space=pltpu.SMEM)
    dma = pltpu.SemaphoreType.DMA
    back, left, right = pl.pallas_call(
        functools.partial(kernel, nf, nx, rows, groups, blocks),
        out_shape=(
            jax.ShapeDtypeStruct((slots, nf, panels, rows, 1, LANES), F32),
            jax.ShapeDtypeStruct(left_stats.shape, F32),
            jax.ShapeDtypeStruct(right_stats.shape, F32),
        ),
        in_specs=[vmem, hbm, hbm, hbm, hbm, hbm],
        out_specs=(vmem, hbm, hbm),
        scratch_shapes=[
            pltpu.VMEM((1, slots * nf), jnp.int32),
            pltpu.SMEM((1, slots * nf), jnp.int32),
            pltpu.VMEM(((blocks + 1) * packet, 1, LANES), F32),
            pltpu.VMEM((slots, nf, panels, rows, 1, LANES), F32),
            pltpu.VMEM((slots, nx, panels, stripe, 1, LANES), F32),
            pltpu.VMEM((slots, panels, stripe, 1, LANES), F32),
            pltpu.VMEM((slots, stripe, width), F32),
            pltpu.VMEM((slots, stripe, width), F32),
            pltpu.VMEM((slots, stripe, width), F32),
            pltpu.VMEM((slots, 3, half, half), F32),
            pltpu.VMEM((slots, 3, half, half), BF16),
            pltpu.VMEM((slots, 3, half, half), BF16),
            pltpu.VMEM((slots, width, width), BF16),
            pltpu.VMEM((slots, width, width), BF16),
            pltpu.VMEM((2 * LANES, width), F32),
            pltpu.VMEM((slots, stripe, width), BF16),
            pltpu.VMEM((slots, stripe, width), BF16),
            pltpu.VMEM((2, stripe, half), BF16),
            pltpu.VMEM((2, stripe, half), BF16),
            pltpu.VMEM((panels, stripe, LANES), F32),
            pltpu.VMEM((slots, nx, 8, LANES), F32),
            dma((9,)),
            dma((4,)),
            dma((slots,)),
            dma((slots, groups)),
            dma((slots, 4)),
            dma((slots, 4)),
            dma((slots, 2, groups)),
            dma((slots, 2, groups)),
            dma((slots, groups)),
            dma((slots, groups)),
            dma((slots, nx - 1)),
            dma((slots, nx - 1)),
            dma((slots,)),
            dma((slots,)),
            pltpu.VMEM((2 * LANES, LANES), F32),
        ],
        compiler_params=pltpu.CompilerParams(
            collective_id=0, has_side_effects=True, vmem_limit_bytes=56 * 1024 * 1024
        ),
    )(owner_slot.reshape(1, blocks), flat, left_root, right_root, left_stats, right_stats)
    update, new_params, new_left, new_right = pl.pallas_call(
        finish,
        out_shape=(
            jax.ShapeDtypeStruct((blocks * packet, LANES), F32),
            jax.ShapeDtypeStruct((rows, blocks, width), BF16),
            jax.ShapeDtypeStruct(left_stats.shape, F32),
            jax.ShapeDtypeStruct(right_stats.shape, F32),
        ),
        in_specs=[smem, vmem, vmem, vmem, vmem],
        out_specs=(vmem, vmem, hbm, hbm),
        scratch_shapes=[pltpu.VMEM((blocks * packet, LANES), F32), dma((2,))],
        compiler_params=pltpu.CompilerParams(vmem_limit_bytes=56 * 1024 * 1024),
    )(owner_slot, back.reshape(slots * nf * packet, LANES), params_t, left, right)
    update = update.reshape(blocks, 1, rows, width)
    new_params = new_params.transpose(1, 0, 2).reshape(blocks, 1, rows, width)
    return (new_params, update, new_left, new_right)


def solution(mesh):
    in_specs = (
        P(None, "rep", "fsdp", None),
        P(None, "rep", "fsdp", None),
        P(),
        P("fsdp", "rep", None),
        P("fsdp", "rep", None),
        P("fsdp", "rep", None),
        P("fsdp", "rep", None),
    )
    out_specs = (
        P(None, "rep", "fsdp", None),
        P(None, "rep", "fsdp", None),
        P("fsdp", "rep", None),
        P("fsdp", "rep", None),
    )
    return jax.shard_map(
        on_device, mesh=mesh, in_specs=in_specs, out_specs=out_specs, check_vma=False
    )
```

```python
import functools

import jax
import jax.numpy as jnp
from jax import lax
from jax.experimental import pallas as pl
from jax.experimental.pallas import tpu as pltpu
from jax.sharding import PartitionSpec as P

STAT_DECAY = 0.95
STEP_SIZE = 0.25
EPSILON = 1e-06
LANES = 128
VIA_MATE = ((2, 4, 6), (1, 3, 5, 7))
F32 = jnp.float32
BF16 = jnp.bfloat16
NN = (((1,), (0,)), ((), ()))
NT = (((1,), (1,)), ((), ()))


def split(value):
    high = value.astype(BF16)
    return high, (value - high.astype(F32)).astype(BF16)


def dot3(left, right, dims):
    dot = functools.partial(lax.dot_general, dimension_numbers=dims, preferred_element_type=F32)
    return dot(left[0], right[0]) + (dot(left[0], right[1]) + dot(left[1], right[0]))


def kernel(
    nf, nx, rows, groups, blocks,
    owner, grads, left_root, right_root, left_stats, right_stats,
    back, scales, new_left, new_right,
    owner_v, blocks_v, slot_block, grads_v, send, gath, ret, left_v, lstat_v, rstat_v,
    root_f, root_h, root_l, gh, gl, gt, lh, ll, mixed, lgh, lgl, sq, scale_v,
    in_sem, a_send, a_recv, r_send, r_recv, x_send, x_recv, f_send, f_recv,
    s_send, s_recv, u_send, u_recv, c_send, c_recv, turned,
):
    slots, stripe, width = left_v.shape
    panels = width // LANES
    half = width // 2
    packet = rows * panels
    size = nf // groups
    chunk = size * rows
    me = lax.axis_index("fsdp")
    x = lax.axis_index("rep")
    mz, mg = me // size, me % size
    right_x, left_x, far_x = (x + 1) % nx, (x + nx - 1) % nx, (x + 2) % nx
    h, pos = x // 2, x % 2
    mate = h * 2 + 1 - pos
    other = jnp.where(pos == 0, left_x, right_x)

    def at_x(target):
        return {"fsdp": me, "rep": target}

    def at_f(target):
        return {"fsdp": target, "rep": x}

    def remote(src, dst, send_sem, recv_sem, device):
        return pltpu.make_async_remote_copy(
            src_ref=src, dst_ref=dst, send_sem=send_sem, recv_sem=recv_sem,
            device_id=device, device_id_type=pl.DeviceIdType.MESH,
        )

    def await_bytes(ref, sem):
        pltpu.make_async_copy(ref, ref, sem).wait()

    order = [0]
    for step in range(groups // 2, 0, -1):
        order.append(step)
        if step != groups - step:
            order.append(groups - step)

    load_grads = pltpu.make_async_copy(grads, grads_v.at[pl.ds(0, blocks * packet)], in_sem.at[0])
    load_grads.start()
    load_owner = pltpu.make_async_copy(owner, owner_v, in_sem.at[9])
    load_owner.start()
    load_left = pltpu.make_async_copy(left_root, left_v, in_sem.at[1])
    load_left.start()
    loads_r = []
    for t in range(slots):
        for kind in range(2):
            col = h if kind == 0 else 1 - h
            cols = pl.ds(pl.multiple_of(col * half, LANES), half)
            src = right_root.at[t, :, cols]
            load = pltpu.make_async_copy(
                src, root_f.at[t, kind, pl.ds(pl.multiple_of(pos * stripe, 8), stripe)], in_sem.at[2 + 2 * t + kind]
            )
            load.start()
            loads_r.append(load)
    load_ls = pltpu.make_async_copy(left_stats, lstat_v, in_sem.at[6])
    load_ls.start()
    load_rs = pltpu.make_async_copy(right_stats, rstat_v, in_sem.at[7])
    load_rs.start()

    barrier = pltpu.get_barrier_semaphore()

    def greet(k, carry):
        pl.semaphore_signal(barrier, inc=1, device_id=at_f((me + k) % nf), device_id_type=pl.DeviceIdType.MESH)
        return carry

    lax.fori_loop(1, nf, greet, 0)
    for d in range(1, nx):
        pl.semaphore_signal(barrier, inc=1, device_id=at_x((x + d) % nx), device_id_type=pl.DeviceIdType.MESH)

    load_owner.wait()
    row = jnp.broadcast_to(owner_v[...], (blocks, blocks))
    down = lax.broadcasted_iota(jnp.int32, (blocks, blocks), 0)
    along = lax.broadcasted_iota(jnp.int32, (blocks, blocks), 1)
    column = jnp.sum(jnp.where(down == along, row, 0), axis=1, keepdims=True)
    slot_ids = lax.broadcasted_iota(jnp.int32, (blocks, slots * nf), 1)
    block_ids = lax.broadcasted_iota(jnp.int32, (blocks, slots * nf), 0)
    held = blocks + jnp.sum(jnp.where(column == slot_ids, block_ids - blocks, 0), axis=0, keepdims=True)
    blocks_v[...] = jnp.maximum(held, 0)
    to_smem = pltpu.make_async_copy(blocks_v, slot_block, in_sem.at[8])
    to_smem.start()
    pl.semaphore_wait(barrier, nf - 1 + nx - 1)

    def diag(t, kind, q):
        return root_f.at[t, kind, pl.ds(pl.multiple_of(q * stripe, 8), stripe), pl.ds(pl.multiple_of(q * LANES, LANES), 2 * LANES)]

    my_rows = pl.ds(pl.multiple_of(pos * stripe, 8), stripe)
    mate_rows = pl.ds(pl.multiple_of((1 - pos) * stripe, 8), stripe)

    def root_copy(t, kind):
        src, dst = (
            (diag(t, 0, pos), diag(t, 0, pos)),
            (root_f.at[t, 1, my_rows], root_f.at[t, 1, my_rows]),
            (root_f.at[t, 0, my_rows], root_f.at[t, 2, my_rows]),
            (diag(t, 0, 1 - pos), diag(t, 2, 1 - pos)),
        )[kind]
        return remote(src, dst, r_send.at[t, kind], r_recv.at[t, kind], at_x(mate if kind < 2 else other))

    def root_arrival(t, kind):
        ref = (
            diag(t, 0, 1 - pos), root_f.at[t, 1, mate_rows], root_f.at[t, 2, mate_rows], diag(t, 2, pos)
        )[kind]
        remote(ref, ref, r_send.at[t, kind], r_recv.at[t, kind], at_x(mate if kind < 2 else other)).wait_recv()

    for t in range(slots):
        loads_r[2 * t].wait()
        loads_r[2 * t + 1].wait()
        root_copy(t, 2).start()
        root_copy(t, 0).start()
        root_copy(t, 1).start()

    load_grads.wait()
    to_smem.wait()
    flat_grads = grads_v.reshape((blocks + 1) * packet, LANES)
    flat_grads[pl.ds(blocks * packet, packet), :] = jnp.zeros((packet, LANES), F32)
    flat_send = send.reshape(slots * nf * packet, LANES)

    def pack(t, dest):
        block = slot_block[0, slots * dest + t]
        for j in range(rows):
            value = flat_grads[pl.ds(block * packet + panels * j, panels), :]
            flat_send[pl.ds((t * nf + dest) * packet + j, panels, stride=rows), :] = value

    for t in range(slots):
        mine = gath.at[t, x, :, pl.ds(me * rows, rows)]
        pack(t, me)
        pltpu.make_async_copy(send.at[t, me], mine, a_recv.at[t, mz]).start()
        for offset in order:
            dz = (mz + offset) % groups

            def post(k, carry, t=t, dz=dz, mine=mine):
                dest = dz * size + (mg + k) % size
                pack(t, dest)
                remote(send.at[t, dest], mine, a_send.at[t], a_recv.at[t, mz], at_f(dest)).start()
                return carry

            lax.fori_loop(1 if offset == 0 else 0, size, post, 0)

    load_left.wait()
    for t in range(slots):
        for i in range(nx):
            lh[t, i], ll[t, i] = split(left_v[t, :, i * stripe : (i + 1) * stripe])

    def rows_of(k):
        source = (mz + groups - order[k]) % groups
        return source, pl.ds(source * chunk, chunk)

    sides = (mate, other)

    def direct(t, k, side):
        source, part = rows_of(k)
        ref = gath.at[t, x, :, part]
        return remote(ref, ref, x_send.at[t, side, k], x_recv.at[t, side, k], at_x(sides[side]))

    def arrival(t, k, side):
        source, part = rows_of(k)
        ref = gath.at[t, sides[side], :, part]
        return remote(ref, ref, x_send.at[t, side, k], x_recv.at[t, side, k], at_x(sides[side]))

    def forward(t, k):
        source, part = rows_of(k)
        to = 0 if k in VIA_MATE[t] else 1
        ref = gath.at[t, sides[1 - to], :, part]
        return remote(ref, ref, f_send.at[t, k], f_recv.at[t, k], at_x(sides[to]))

    def far_arrival(t, k):
        source, part = rows_of(k)
        ref = gath.at[t, far_x, :, part]
        return remote(ref, ref, f_send.at[t, k], f_recv.at[t, k], at_x(mate))

    def spread(t):
        for k in range(groups):
            source, part = rows_of(k)
            await_bytes(gath.at[t, x, :, part], a_recv.at[t, source])
            direct(t, k, 0).start()
            direct(t, k, 1).start()

    def relay(t):
        for k in range(groups):
            arrival(t, k, 1 if k in VIA_MATE[t] else 0).wait_recv()
            forward(t, k).start()

    def gather_rest(t):
        for k in range(groups):
            arrival(t, k, 0 if k in VIA_MATE[t] else 1).wait_recv()

    g4 = gath.reshape(slots, nx, panels, stripe, LANES)
    ret4 = ret.reshape(slots, panels, stripe, LANES)

    def take(t, i):
        total = jnp.zeros((1, LANES), F32)
        part = pl.ds(pl.multiple_of(i * stripe, 16), stripe)
        for c in range(panels):
            value = g4[t, i, c]
            total = total + jnp.sum(value * value, axis=0, keepdims=True)
            high, low = split(value)
            gh[t, part, c * LANES : (c + 1) * LANES] = high
            gl[t, part, c * LANES : (c + 1) * LANES] = low
        return total

    def mix(t, i, place):
        part = pl.ds(pl.multiple_of(i * stripe, 16), stripe)
        for c in range(2):
            cols = slice(c * half, (c + 1) * half)
            term = dot3((lh[t, i], ll[t, i]), (gh[t, part, cols], gl[t, part, cols]), NN)
            if place == 0:
                mixed[c] = term
            elif place < nx - 1:
                mixed[c] = mixed[c] + term
            else:
                lgh[c], lgl[c] = split(mixed[c] + term)

    per = half // LANES

    def precondition(t, near_part):
        near = (lgh[h], lgl[h])
        away = (lgh[1 - h], lgl[1 - h])
        root = [(root_h[t, kind], root_l[t, kind]) for kind in range(3)]
        if near_part:
            part = dot3(near, root[0], NN) + dot3(away, root[1], NT)
        else:
            part = dot3(near, root[1], NN) + dot3(away, root[2], NN)
        first = (h if near_part else 1 - h) * per
        for c in range(per):
            ret4[t, first + c] = part[:, c * LANES : (c + 1) * LANES]
        return jnp.sum(part * part, axis=0, keepdims=True)

    def square_send(t, squares):
        sq[t, x] = jnp.broadcast_to(jnp.sum(squares, axis=1, keepdims=True), sq.shape[2:])
        for d in range(1, nx):
            remote(sq.at[t, x], sq.at[t, x], s_send.at[t, d - 1], s_recv.at[t, d - 1], at_x((x + d) % nx)).start()

    def scale_of(t, grad_squares):
        for d in range(1, nx):
            ref = sq.at[t, (x + nx - d) % nx]
            remote(ref, ref, s_send.at[t, d - 1], s_recv.at[t, d - 1], at_x((x + d) % nx)).wait_recv()
        prec_mean = (((sq[t, 0] + sq[t, 1]) + sq[t, 2]) + sq[t, 3]) / (width * width)
        grad_mean = jnp.sum(grad_squares, axis=1, keepdims=True) / (width * width)
        scale_v[t] = jnp.sqrt(grad_mean / (prec_mean[0:1, :] + EPSILON))

    def to_all(post):
        for offset in order[1:] + order[:1]:
            dz = (mz + offset) % groups

            def body(k, carry, dz=dz):
                post(dz * size + (mg + k) % size)
                return carry

            lax.fori_loop(1 if offset == 0 else 0, size, body, 0)

    def give_back(t, part, first, count):
        span = pl.ds(first, count)

        def post(dest):
            src = ret.at[t, span, pl.ds(dest * rows, rows)]
            remote(src, back.at[t, me, span], u_send.at[part], u_recv.at[part], at_f(dest)).start()

        own = ret.at[t, span, pl.ds(me * rows, rows)]
        pltpu.make_async_copy(own, back.at[t, me, span], u_recv.at[part]).start()
        to_all(post)

    def give_scales():
        pltpu.make_async_copy(scale_v, scales.at[me], c_recv).start()
        to_all(lambda dest: remote(scale_v, scales.at[me], c_send, c_recv, at_f(dest)).start())

    def left_gram(t):
        mine = pl.ds(pl.multiple_of(x * stripe, 16), stripe)
        ours = (gh[t, mine], gl[t, mine])
        for n in range(3):
            part = slice(n * 256, (n + 1) * 256)
            gram = dot3(ours, (gh[t, part], gl[t, part]), NT)
            new_left[t, :, part] = STAT_DECAY * lstat_v[t, :, part] + (1.0 - STAT_DECAY) * gram

    def right_gram(t):
        first = (3 * x) // 2
        for i in range(nx):
            pair = jnp.concatenate([g4[t, i, first], g4[t, i, first + 1]], axis=1)
            gt[:, i * stripe : (i + 1) * stripe] = pair.T
        ours = split(gt[pl.ds(pl.multiple_of(pos * (LANES // 2), 8), stripe), :])
        for n in range(3):
            part = slice(n * 256, (n + 1) * 256)
            gram = dot3(ours, (gh[t, :, part], gl[t, :, part]), NN)
            new_right[t, :, part] = STAT_DECAY * rstat_v[t, :, part] + (1.0 - STAT_DECAY) * gram

    def mirror(t, kind, q):
        panel = pl.ds(pl.multiple_of((1 - q) * 2 * LANES, LANES), LANES)
        wide = root_f[t, kind, panel, pl.ds(pl.multiple_of(q * LANES, LANES), 2 * LANES)]
        turned[...] = wide.T
        part = turned[pl.ds(pl.multiple_of(q * (LANES // 2), 8), stripe), :]
        root_f[t, kind, pl.ds(pl.multiple_of(q * stripe, 8), stripe), panel] = part

    def take_root(t, kind):
        root_h[t, kind], root_l[t, kind] = split(root_f[t, kind])

    totals = [None] * slots
    root_arrival(0, 0)
    root_copy(0, 3).start()
    spread(0)
    root_arrival(0, 1)
    mirror(0, 0, 1 - pos)
    take_root(0, 0)
    take_root(0, 1)
    relay(0)
    spread(1)
    root_arrival(0, 2)
    root_arrival(0, 3)
    mirror(0, 2, pos)
    take_root(0, 2)
    totals[0] = take(0, x)
    mix(0, x, 0)
    gather_rest(0)
    for place, i in ((1, mate), (2, other)):
        totals[0] = totals[0] + take(0, i)
        mix(0, i, place)
    for k in range(groups):
        far_arrival(0, k).wait_recv()
    totals[0] = totals[0] + take(0, far_x)
    mix(0, far_x, 3)
    square_send(0, precondition(0, True) + precondition(0, False))
    give_back(0, 0, 0, panels)
    relay(1)
    root_arrival(1, 0)
    root_copy(1, 3).start()
    root_arrival(1, 1)
    mirror(1, 0, 1 - pos)
    take_root(1, 0)
    take_root(1, 1)
    scale_of(0, totals[0])
    load_ls.wait()
    left_gram(0)
    totals[1] = take(1, x)
    mix(1, x, 0)
    gather_rest(1)
    for place, i in ((1, mate), (2, other)):
        totals[1] = totals[1] + take(1, i)
        mix(1, i, place)
    for k in range(groups):
        far_arrival(1, k).wait_recv()
    totals[1] = totals[1] + take(1, far_x)
    mix(1, far_x, 3)
    squares = precondition(1, True)
    give_back(1, 1, h * per, per)
    root_arrival(1, 2)
    root_arrival(1, 3)
    mirror(1, 2, pos)
    take_root(1, 2)
    square_send(1, squares + precondition(1, False))
    give_back(1, 2, (1 - h) * per, per)
    scale_of(1, totals[1])
    give_scales()
    load_rs.wait()
    right_gram(0)
    left_gram(1)
    right_gram(1)
    await_bytes(back.at[0], u_recv.at[0])
    await_bytes(back.at[1, :, pl.ds(h * per, per)], u_recv.at[1])
    await_bytes(back.at[1, :, pl.ds((1 - h) * per, per)], u_recv.at[2])
    await_bytes(scales, c_recv)

    for t in range(slots):
        await_bytes(send.at[t, pl.ds(0, nf - 1)], a_send.at[t])
        for k in range(groups):
            direct(t, k, 0).wait_send()
            direct(t, k, 1).wait_send()
            forward(t, k).wait_send()
        for d in range(1, nx):
            remote(sq.at[t, x], sq.at[t, x], s_send.at[t, d - 1], s_recv.at[t, d - 1], at_x((x + d) % nx)).wait_send()
        for kind in range(4):
            root_copy(t, kind).wait_send()
    await_bytes(back.at[0, pl.ds(0, nf - 1)], u_send.at[0])
    await_bytes(back.at[1, pl.ds(0, nf - 1), pl.ds(0, per)], u_send.at[1])
    await_bytes(back.at[1, pl.ds(0, nf - 1), pl.ds(0, per)], u_send.at[2])
    await_bytes(scales.at[pl.ds(0, nf - 1)], c_send)


def finish(owner, back, scales, params, left, right, update, new_params, new_left, new_right, upd_t, sem):
    moves = (pltpu.make_async_copy(left, new_left, sem.at[0]), pltpu.make_async_copy(right, new_right, sem.at[1]))
    for move in moves:
        move.start()
    rows, blocks, width = params.shape
    panels = width // LANES
    packet = rows * panels
    slots = left.shape[0]
    nf = back.shape[0] // (packet * slots)

    def place(b, carry):
        slot = owner[b]
        start = ((slot % slots) * nf + slot // slots) * packet
        scale = scales[pl.ds(slot, 1), :]
        for c in range(panels):
            value = back[pl.ds(start + rows * c, rows), :] * scale
            update[pl.ds(b * packet + c, rows, stride=panels), :] = value
            upd_t[pl.ds(c * blocks + b, rows, stride=panels * blocks), :] = value
        return carry

    lax.fori_loop(0, blocks, place, 0, unroll=4)
    for j in range(rows):
        for c in range(panels):
            cols = slice(c * LANES, (c + 1) * LANES)
            step = STEP_SIZE * upd_t[(j * panels + c) * blocks : (j * panels + c + 1) * blocks, :]
            new_params[j, :, cols] = (params[j, :, cols].astype(F32) - step).astype(BF16)
    for move in moves:
        move.wait()


def on_device(grads, params, owner_slot, left_stats, right_stats, left_root, right_root):
    blocks, _, rows, width = grads.shape
    nf = lax.axis_size("fsdp")
    nx = lax.axis_size("rep")
    slots, stripe, _ = left_stats.shape
    panels = width // LANES
    half = width // 2
    packet = rows * panels
    groups = 8 if nf >= 64 else 2
    flat = grads.reshape(blocks * packet, 1, LANES)
    params_t = params.reshape(blocks, rows, width).transpose(1, 0, 2)
    hbm = pl.BlockSpec(memory_space=pltpu.HBM)
    vmem = pl.BlockSpec(memory_space=pltpu.VMEM)
    smem = pl.BlockSpec(memory_space=pltpu.SMEM)
    dma = pltpu.SemaphoreType.DMA
    back, scales, left, right = pl.pallas_call(
        functools.partial(kernel, nf, nx, rows, groups, blocks),
        out_shape=(
            pltpu.VMEM((slots, nf, panels, rows, 1, LANES), F32),
            pltpu.VMEM((nf, slots, 1, LANES), F32),
            pltpu.VMEM(left_stats.shape, F32),
            pltpu.VMEM(right_stats.shape, F32),
        ),
        in_specs=[hbm, hbm, hbm, hbm, hbm, hbm],
        out_specs=(vmem, vmem, vmem, vmem),
        scratch_shapes=[
            pltpu.VMEM((1, blocks), jnp.int32),
            pltpu.VMEM((1, slots * nf), jnp.int32),
            pltpu.SMEM((1, slots * nf), jnp.int32),
            pltpu.VMEM(((blocks + 1) * packet, 1, LANES), F32),
            pltpu.VMEM((slots, nf, panels, rows, 1, LANES), F32),
            pltpu.VMEM((slots, nx, panels, stripe, 1, LANES), F32),
            pltpu.VMEM((slots, panels, stripe, 1, LANES), F32),
            pltpu.VMEM((slots, stripe, width), F32),
            pltpu.VMEM((slots, stripe, width), F32),
            pltpu.VMEM((slots, stripe, width), F32),
            pltpu.VMEM((slots, 3, half, half), F32),
            pltpu.VMEM((slots, 3, half, half), BF16),
            pltpu.VMEM((slots, 3, half, half), BF16),
            pltpu.VMEM((slots, width, width), BF16),
            pltpu.VMEM((slots, width, width), BF16),
            pltpu.VMEM((2 * LANES, width), F32),
            pltpu.VMEM((slots, nx, stripe, stripe), BF16),
            pltpu.VMEM((slots, nx, stripe, stripe), BF16),
            pltpu.VMEM((2, stripe, half), F32),
            pltpu.VMEM((2, stripe, half), BF16),
            pltpu.VMEM((2, stripe, half), BF16),
            pltpu.VMEM((slots, nx, 8, LANES), F32),
            pltpu.VMEM((slots, 1, LANES), F32),
            dma((10,)),
            dma((slots,)),
            dma((slots, groups)),
            dma((slots, 4)),
            dma((slots, 4)),
            dma((slots, 2, groups)),
            dma((slots, 2, groups)),
            dma((slots, groups)),
            dma((slots, groups)),
            dma((slots, nx - 1)),
            dma((slots, nx - 1)),
            dma((3,)),
            dma((3,)),
            dma(()),
            dma(()),
            pltpu.VMEM((2 * LANES, LANES), F32),
        ],
        compiler_params=pltpu.CompilerParams(
            collective_id=0, has_side_effects=True, vmem_limit_bytes=60 * 1024 * 1024
        ),
    )(owner_slot.reshape(1, blocks), flat, left_root, right_root, left_stats, right_stats)
    update, new_params, new_left, new_right = pl.pallas_call(
        finish,
        out_shape=(
            jax.ShapeDtypeStruct((blocks * packet, LANES), F32),
            jax.ShapeDtypeStruct((rows, blocks, width), BF16),
            jax.ShapeDtypeStruct(left_stats.shape, F32),
            jax.ShapeDtypeStruct(right_stats.shape, F32),
        ),
        in_specs=[smem, vmem, vmem, vmem, vmem, vmem],
        out_specs=(vmem, vmem, hbm, hbm),
        scratch_shapes=[
            pltpu.VMEM((blocks * packet, LANES), F32),
            dma((2,)),
        ],
        compiler_params=pltpu.CompilerParams(vmem_limit_bytes=16 * 1024 * 1024),
    )(owner_slot, back.reshape(slots * nf * packet, LANES), scales.reshape(nf * slots, LANES), params_t, left, right)
    update = update.reshape(blocks, 1, rows, width)
    new_params = new_params.transpose(1, 0, 2).reshape(blocks, 1, rows, width)
    return (new_params, update, new_left, new_right)


def solution(mesh):
    in_specs = (
        P(None, "rep", "fsdp", None),
        P(None, "rep", "fsdp", None),
        P(),
        P("fsdp", "rep", None),
        P("fsdp", "rep", None),
        P("fsdp", "rep", None),
        P("fsdp", "rep", None),
    )
    out_specs = (
        P(None, "rep", "fsdp", None),
        P(None, "rep", "fsdp", None),
        P("fsdp", "rep", None),
        P("fsdp", "rep", None),
    )
    return jax.shard_map(
        on_device, mesh=mesh, in_specs=in_specs, out_specs=out_specs, check_vma=False
    )
```

```python
import functools

import jax
import jax.numpy as jnp
from jax import lax
from jax.experimental import pallas as pl
from jax.experimental.pallas import tpu as pltpu
from jax.sharding import PartitionSpec as P

STAT_DECAY = 0.95
STEP_SIZE = 0.25
EPSILON = 1e-06
LANES = 128
VIA_MATE = ((2, 4, 6), (1, 3, 5, 7))
F32 = jnp.float32
BF16 = jnp.bfloat16
NN = (((1,), (0,)), ((), ()))
NT = (((1,), (1,)), ((), ()))


def split(value):
    high = value.astype(BF16)
    return high, (value - high.astype(F32)).astype(BF16)


def dot3(left, right, dims):
    dot = functools.partial(lax.dot_general, dimension_numbers=dims, preferred_element_type=F32)
    return dot(left[0], right[0]) + (dot(left[0], right[1]) + dot(left[1], right[0]))


def kernel(
    nf, nx, rows, groups, blocks,
    owner, grads, left_root, right_root, left_stats, right_stats,
    back, scales, new_left, new_right,
    owner_v, blocks_v, slot_block, grads_v, send, last, send_last, gath, ret, left_v, lstat_v, rstat_v,
    root_f, root_h, root_l, gh, gl, gt, lh, ll, mixed, lgh, lgl, sq, scale_v,
    in_sem, a_send, a_recv, r_send, r_recv, x_send, x_recv, f_send, f_recv,
    s_send, s_recv, u_send, u_recv, c_send, c_recv, q_send, q_recv, p_send, p_recv, turned,
):
    slots, stripe, width = left_v.shape
    panels = width // LANES
    half = width // 2
    packet = rows * panels
    front = panels - 1
    sent = rows * front
    size = nf // groups
    chunk = size * rows
    me = lax.axis_index("fsdp")
    x = lax.axis_index("rep")
    mz, mg = me // size, me % size
    right_x, left_x, far_x = (x + 1) % nx, (x + nx - 1) % nx, (x + 2) % nx
    h, pos = x // 2, x % 2
    mate = h * 2 + 1 - pos
    other = jnp.where(pos == 0, left_x, right_x)

    def at_x(target):
        return {"fsdp": me, "rep": target}

    def at_f(target):
        return {"fsdp": target, "rep": x}

    def remote(src, dst, send_sem, recv_sem, device):
        return pltpu.make_async_remote_copy(
            src_ref=src, dst_ref=dst, send_sem=send_sem, recv_sem=recv_sem,
            device_id=device, device_id_type=pl.DeviceIdType.MESH,
        )

    def await_bytes(ref, sem):
        pltpu.make_async_copy(ref, ref, sem).wait()

    order = [0]
    for step in range(groups // 2, 0, -1):
        order.append(step)
        if step != groups - step:
            order.append(groups - step)

    load_grads = pltpu.make_async_copy(grads, grads_v.at[pl.ds(0, blocks * packet)], in_sem.at[0])
    load_grads.start()
    load_owner = pltpu.make_async_copy(owner, owner_v, in_sem.at[9])
    load_owner.start()
    load_left = pltpu.make_async_copy(left_root, left_v, in_sem.at[1])
    load_left.start()
    loads_r = []
    for t in range(slots):
        for kind in range(2):
            col = h if kind == 0 else 1 - h
            cols = pl.ds(pl.multiple_of(col * half, LANES), half)
            src = right_root.at[t, :, cols]
            load = pltpu.make_async_copy(
                src, root_f.at[t, kind, pl.ds(pl.multiple_of(pos * stripe, 8), stripe)], in_sem.at[2 + 2 * t + kind]
            )
            load.start()
            loads_r.append(load)
    load_ls = pltpu.make_async_copy(left_stats, lstat_v, in_sem.at[6])
    load_ls.start()
    load_rs = pltpu.make_async_copy(right_stats, rstat_v, in_sem.at[7])
    load_rs.start()

    barrier = pltpu.get_barrier_semaphore()

    def greet(k, carry):
        pl.semaphore_signal(barrier, inc=1, device_id=at_f((me + k) % nf), device_id_type=pl.DeviceIdType.MESH)
        return carry

    lax.fori_loop(1, nf, greet, 0)
    for d in range(1, nx):
        pl.semaphore_signal(barrier, inc=1, device_id=at_x((x + d) % nx), device_id_type=pl.DeviceIdType.MESH)

    load_owner.wait()
    row = jnp.broadcast_to(owner_v[...], (blocks, blocks))
    down = lax.broadcasted_iota(jnp.int32, (blocks, blocks), 0)
    along = lax.broadcasted_iota(jnp.int32, (blocks, blocks), 1)
    column = jnp.sum(jnp.where(down == along, row, 0), axis=1, keepdims=True)
    slot_ids = lax.broadcasted_iota(jnp.int32, (blocks, slots * nf), 1)
    block_ids = lax.broadcasted_iota(jnp.int32, (blocks, slots * nf), 0)
    held = blocks + jnp.sum(jnp.where(column == slot_ids, block_ids - blocks, 0), axis=0, keepdims=True)
    blocks_v[...] = jnp.maximum(held, 0)
    to_smem = pltpu.make_async_copy(blocks_v, slot_block, in_sem.at[8])
    to_smem.start()
    load_grads.wait()
    flat_grads = grads_v.reshape((blocks + 1) * packet, LANES)
    flat_grads[pl.ds(blocks * packet, packet), :] = jnp.zeros((packet, LANES), F32)
    flat_last = last.reshape(nx * (blocks + 1) * rows, LANES)
    for i in range(nx):
        flat_last[pl.ds((i * (blocks + 1) + blocks) * rows, rows), :] = jnp.zeros((rows, LANES), F32)
    own_last = flat_grads[pl.ds(front, blocks * rows, stride=panels), :]
    flat_last[pl.ds(x * (blocks + 1) * rows, blocks * rows), :] = own_last
    pl.semaphore_wait(barrier, nf - 1 + nx - 1)

    def diag(t, kind, q):
        return root_f.at[t, kind, pl.ds(pl.multiple_of(q * stripe, 8), stripe), pl.ds(pl.multiple_of(q * LANES, LANES), 2 * LANES)]

    my_rows = pl.ds(pl.multiple_of(pos * stripe, 8), stripe)
    mate_rows = pl.ds(pl.multiple_of((1 - pos) * stripe, 8), stripe)

    def root_copy(t, kind):
        src, dst = (
            (diag(t, 0, pos), diag(t, 0, pos)),
            (root_f.at[t, 1, my_rows], root_f.at[t, 1, my_rows]),
            (root_f.at[t, 0, my_rows], root_f.at[t, 2, my_rows]),
            (diag(t, 0, 1 - pos), diag(t, 2, 1 - pos)),
        )[kind]
        return remote(src, dst, r_send.at[t, kind], r_recv.at[t, kind], at_x(mate if kind < 2 else other))

    def root_arrival(t, kind):
        ref = (
            diag(t, 0, 1 - pos), root_f.at[t, 1, mate_rows], root_f.at[t, 2, mate_rows], diag(t, 2, pos)
        )[kind]
        remote(ref, ref, r_send.at[t, kind], r_recv.at[t, kind], at_x(mate if kind < 2 else other)).wait_recv()

    span = blocks * rows
    low, high = pl.ds(0, span // 2), pl.ds(span // 2, span // 2)

    def last_copy(kind):
        ref = (last.at[x, pl.ds(0, span)], last.at[x, pl.ds(0, span)], last.at[other, low], last.at[mate, high])[kind]
        return remote(ref, ref, q_send.at[kind], q_recv.at[kind], at_x(mate if kind % 2 == 0 else other))

    def last_arrival(kind):
        ref = (last.at[mate, pl.ds(0, span)], last.at[other, pl.ds(0, span)], last.at[far_x, low], last.at[far_x, high])[kind]
        remote(ref, ref, q_send.at[kind], q_recv.at[kind], at_x(mate if kind % 2 == 0 else other)).wait_recv()

    last_copy(0).start()
    last_copy(1).start()
    for t in range(slots):
        loads_r[2 * t].wait()
        loads_r[2 * t + 1].wait()
        root_copy(t, 2).start()
        root_copy(t, 0).start()
        root_copy(t, 1).start()

    to_smem.wait()
    flat_send = send.reshape(slots * nf * sent, LANES)
    flat_send_last = send_last.reshape(slots * nf * nx * rows, LANES)

    def pack(t, dest):
        block = slot_block[0, slots * dest + t]
        for j in range(rows):
            value = flat_grads[pl.ds(block * packet + panels * j, front), :]
            flat_send[pl.ds((t * nf + dest) * sent + j, front, stride=rows), :] = value

    def pack_last(t, dest):
        block = slot_block[0, slots * dest + t]
        for i in range(nx):
            value = flat_last[pl.ds((i * (blocks + 1) + block) * rows, rows), :]
            flat_send_last[pl.ds(((t * nf + dest) * nx + i) * rows, rows), :] = value

    def give_rows(t):
        mine = gath.at[t, x, pl.ds(0, front), pl.ds(me * rows, rows)]
        pack(t, me)
        pltpu.make_async_copy(send.at[t, me], mine, a_recv.at[t, mz]).start()
        for offset in order:
            dz = (mz + offset) % groups

            def post(k, carry, dz=dz):
                dest = dz * size + (mg + k) % size
                pack(t, dest)
                remote(send.at[t, dest], mine, a_send.at[t], a_recv.at[t, mz], at_f(dest)).start()
                return carry

            lax.fori_loop(1 if offset == 0 else 0, size, post, 0)

    def give_last(t):
        mine = gath.at[t, :, front, pl.ds(me * rows, rows)]
        pack_last(t, me)
        pltpu.make_async_copy(send_last.at[t, me], mine, p_recv.at[t]).start()
        for offset in order:
            dz = (mz + offset) % groups

            def post(k, carry, dz=dz):
                dest = dz * size + (mg + k) % size
                pack_last(t, dest)
                remote(send_last.at[t, dest], mine, p_send.at[t], p_recv.at[t], at_f(dest)).start()
                return carry

            lax.fori_loop(1 if offset == 0 else 0, size, post, 0)

    def split_left():
        load_left.wait()
        for t in range(slots):
            for i in range(nx):
                lh[t, i], ll[t, i] = split(left_v[t, :, i * stripe : (i + 1) * stripe])


    def rows_of(k):
        source = (mz + groups - order[k]) % groups
        return source, pl.ds(source * chunk, chunk)

    sides = (mate, other)

    def direct(t, k, side):
        source, part = rows_of(k)
        ref = gath.at[t, x, pl.ds(0, front), part]
        return remote(ref, ref, x_send.at[t, side, k], x_recv.at[t, side, k], at_x(sides[side]))

    def arrival(t, k, side):
        source, part = rows_of(k)
        ref = gath.at[t, sides[side], pl.ds(0, front), part]
        return remote(ref, ref, x_send.at[t, side, k], x_recv.at[t, side, k], at_x(sides[side]))

    def forward(t, k):
        source, part = rows_of(k)
        to = 0 if k in VIA_MATE[t] else 1
        ref = gath.at[t, sides[1 - to], pl.ds(0, front), part]
        return remote(ref, ref, f_send.at[t, k], f_recv.at[t, k], at_x(sides[to]))

    def far_arrival(t, k):
        source, part = rows_of(k)
        ref = gath.at[t, far_x, pl.ds(0, front), part]
        return remote(ref, ref, f_send.at[t, k], f_recv.at[t, k], at_x(mate))

    def spread(t):
        for k in range(groups):
            source, part = rows_of(k)
            await_bytes(gath.at[t, x, pl.ds(0, front), part], a_recv.at[t, source])
            direct(t, k, 0).start()
            direct(t, k, 1).start()

    def relay(t):
        for k in range(groups):
            arrival(t, k, 1 if k in VIA_MATE[t] else 0).wait_recv()
            forward(t, k).start()

    def gather_rest(t):
        for k in range(groups):
            arrival(t, k, 0 if k in VIA_MATE[t] else 1).wait_recv()

    g4 = gath.reshape(slots, nx, panels, stripe, LANES)
    ret4 = ret.reshape(slots, panels, stripe, LANES)

    def take(t, i):
        total = jnp.zeros((1, LANES), F32)
        part = pl.ds(pl.multiple_of(i * stripe, 16), stripe)
        for c in range(panels):
            value = g4[t, i, c]
            total = total + jnp.sum(value * value, axis=0, keepdims=True)
            high, low = split(value)
            gh[t, part, c * LANES : (c + 1) * LANES] = high
            gl[t, part, c * LANES : (c + 1) * LANES] = low
        return total

    def mix(t, i, place):
        part = pl.ds(pl.multiple_of(i * stripe, 16), stripe)
        for c in range(2):
            cols = slice(c * half, (c + 1) * half)
            term = dot3((lh[t, i], ll[t, i]), (gh[t, part, cols], gl[t, part, cols]), NN)
            if place == 0:
                mixed[c] = term
            elif place < nx - 1:
                mixed[c] = mixed[c] + term
            else:
                lgh[c], lgl[c] = split(mixed[c] + term)

    per = half // LANES

    def precondition(t, near_part):
        near = (lgh[h], lgl[h])
        away = (lgh[1 - h], lgl[1 - h])
        root = [(root_h[t, kind], root_l[t, kind]) for kind in range(3)]
        if near_part:
            part = dot3(near, root[0], NN) + dot3(away, root[1], NT)
        else:
            part = dot3(near, root[1], NN) + dot3(away, root[2], NN)
        first = (h if near_part else 1 - h) * per
        for c in range(per):
            ret4[t, first + c] = part[:, c * LANES : (c + 1) * LANES]
        return jnp.sum(part * part, axis=0, keepdims=True)

    def square_send(t, squares):
        sq[t, x] = jnp.broadcast_to(jnp.sum(squares, axis=1, keepdims=True), sq.shape[2:])
        for d in range(1, nx):
            remote(sq.at[t, x], sq.at[t, x], s_send.at[t, d - 1], s_recv.at[t, d - 1], at_x((x + d) % nx)).start()

    def scale_of(t, grad_squares):
        for d in range(1, nx):
            ref = sq.at[t, (x + nx - d) % nx]
            remote(ref, ref, s_send.at[t, d - 1], s_recv.at[t, d - 1], at_x((x + d) % nx)).wait_recv()
        prec_mean = (((sq[t, 0] + sq[t, 1]) + sq[t, 2]) + sq[t, 3]) / (width * width)
        grad_mean = jnp.sum(grad_squares, axis=1, keepdims=True) / (width * width)
        scale_v[t] = jnp.sqrt(grad_mean / (prec_mean[0:1, :] + EPSILON))

    def to_all(post):
        for offset in order[1:] + order[:1]:
            dz = (mz + offset) % groups

            def body(k, carry, dz=dz):
                post(dz * size + (mg + k) % size)
                return carry

            lax.fori_loop(1 if offset == 0 else 0, size, body, 0)

    def give_back(t, part, first, count):
        span = pl.ds(first, count)

        def post(dest):
            src = ret.at[t, span, pl.ds(dest * rows, rows)]
            remote(src, back.at[t, me, span], u_send.at[part], u_recv.at[part], at_f(dest)).start()

        own = ret.at[t, span, pl.ds(me * rows, rows)]
        pltpu.make_async_copy(own, back.at[t, me, span], u_recv.at[part]).start()
        to_all(post)

    def give_scales():
        pltpu.make_async_copy(scale_v, scales.at[me], c_recv).start()
        to_all(lambda dest: remote(scale_v, scales.at[me], c_send, c_recv, at_f(dest)).start())

    def left_gram(t):
        mine = pl.ds(pl.multiple_of(x * stripe, 16), stripe)
        ours = (gh[t, mine], gl[t, mine])
        for n in range(3):
            part = slice(n * 256, (n + 1) * 256)
            gram = dot3(ours, (gh[t, part], gl[t, part]), NT)
            new_left[t, :, part] = STAT_DECAY * lstat_v[t, :, part] + (1.0 - STAT_DECAY) * gram

    def right_gram(t):
        first = (3 * x) // 2
        for i in range(nx):
            pair = jnp.concatenate([g4[t, i, first], g4[t, i, first + 1]], axis=1)
            gt[:, i * stripe : (i + 1) * stripe] = pair.T
        ours = split(gt[pl.ds(pl.multiple_of(pos * (LANES // 2), 8), stripe), :])
        for n in range(3):
            part = slice(n * 256, (n + 1) * 256)
            gram = dot3(ours, (gh[t, :, part], gl[t, :, part]), NN)
            new_right[t, :, part] = STAT_DECAY * rstat_v[t, :, part] + (1.0 - STAT_DECAY) * gram

    def mirror(t, kind, q):
        panel = pl.ds(pl.multiple_of((1 - q) * 2 * LANES, LANES), LANES)
        wide = root_f[t, kind, panel, pl.ds(pl.multiple_of(q * LANES, LANES), 2 * LANES)]
        turned[...] = wide.T
        part = turned[pl.ds(pl.multiple_of(q * (LANES // 2), 8), stripe), :]
        root_f[t, kind, pl.ds(pl.multiple_of(q * stripe, 8), stripe), panel] = part

    def take_root(t, kind):
        root_h[t, kind], root_l[t, kind] = split(root_f[t, kind])

    totals = [None] * slots
    give_rows(0)
    for kind in range(2):
        last_arrival(kind)
    for kind in range(2, 4):
        last_copy(kind).start()
    root_arrival(0, 0)
    root_copy(0, 3).start()
    give_rows(1)
    split_left()
    spread(0)
    for kind in range(2, 4):
        last_arrival(kind)
    give_last(0)
    root_arrival(0, 1)
    mirror(0, 0, 1 - pos)
    take_root(0, 0)
    take_root(0, 1)
    relay(0)
    spread(1)
    give_last(1)
    root_arrival(0, 2)
    root_arrival(0, 3)
    mirror(0, 2, pos)
    take_root(0, 2)
    await_bytes(gath.at[0, :, front], p_recv.at[0])
    totals[0] = take(0, x)
    mix(0, x, 0)
    gather_rest(0)
    for place, i in ((1, mate), (2, other)):
        totals[0] = totals[0] + take(0, i)
        mix(0, i, place)
    for k in range(groups):
        far_arrival(0, k).wait_recv()
    totals[0] = totals[0] + take(0, far_x)
    mix(0, far_x, 3)
    square_send(0, precondition(0, True) + precondition(0, False))
    give_back(0, 0, 0, panels)
    relay(1)
    root_arrival(1, 0)
    root_copy(1, 3).start()
    root_arrival(1, 1)
    mirror(1, 0, 1 - pos)
    take_root(1, 0)
    take_root(1, 1)
    scale_of(0, totals[0])
    load_ls.wait()
    left_gram(0)
    await_bytes(gath.at[1, :, front], p_recv.at[1])
    totals[1] = take(1, x)
    mix(1, x, 0)
    gather_rest(1)
    for place, i in ((1, mate), (2, other)):
        totals[1] = totals[1] + take(1, i)
        mix(1, i, place)
    for k in range(groups):
        far_arrival(1, k).wait_recv()
    totals[1] = totals[1] + take(1, far_x)
    mix(1, far_x, 3)
    squares = precondition(1, True)
    give_back(1, 1, h * per, per)
    root_arrival(1, 2)
    root_arrival(1, 3)
    mirror(1, 2, pos)
    take_root(1, 2)
    square_send(1, squares + precondition(1, False))
    give_back(1, 2, (1 - h) * per, per)
    scale_of(1, totals[1])
    give_scales()
    load_rs.wait()
    right_gram(0)
    left_gram(1)
    right_gram(1)
    await_bytes(back.at[0], u_recv.at[0])
    await_bytes(back.at[1, :, pl.ds(h * per, per)], u_recv.at[1])
    await_bytes(back.at[1, :, pl.ds((1 - h) * per, per)], u_recv.at[2])
    await_bytes(scales, c_recv)

    for t in range(slots):
        await_bytes(send.at[t, pl.ds(0, nf - 1)], a_send.at[t])
        for k in range(groups):
            direct(t, k, 0).wait_send()
            direct(t, k, 1).wait_send()
            forward(t, k).wait_send()
        for d in range(1, nx):
            remote(sq.at[t, x], sq.at[t, x], s_send.at[t, d - 1], s_recv.at[t, d - 1], at_x((x + d) % nx)).wait_send()
        for kind in range(4):
            root_copy(t, kind).wait_send()
    await_bytes(back.at[0, pl.ds(0, nf - 1)], u_send.at[0])
    await_bytes(back.at[1, pl.ds(0, nf - 1), pl.ds(0, per)], u_send.at[1])
    await_bytes(back.at[1, pl.ds(0, nf - 1), pl.ds(0, per)], u_send.at[2])
    await_bytes(scales.at[pl.ds(0, nf - 1)], c_send)
    for kind in range(4):
        last_copy(kind).wait_send()
    for t in range(slots):
        await_bytes(send_last.at[t, pl.ds(0, nf - 1)], p_send.at[t])


def finish(owner, back, scales, params, left, right, update, new_params, new_left, new_right, upd_t, sem):
    moves = (pltpu.make_async_copy(left, new_left, sem.at[0]), pltpu.make_async_copy(right, new_right, sem.at[1]))
    for move in moves:
        move.start()
    rows, blocks, width = params.shape
    panels = width // LANES
    packet = rows * panels
    slots = left.shape[0]
    nf = back.shape[0] // (packet * slots)

    def place(b, carry):
        slot = owner[b]
        start = ((slot % slots) * nf + slot // slots) * packet
        scale = scales[pl.ds(slot, 1), :]
        for c in range(panels):
            value = back[pl.ds(start + rows * c, rows), :] * scale
            update[pl.ds(b * packet + c, rows, stride=panels), :] = value
            upd_t[pl.ds(c * blocks + b, rows, stride=panels * blocks), :] = value
        return carry

    lax.fori_loop(0, blocks, place, 0, unroll=4)
    for j in range(rows):
        for c in range(panels):
            cols = slice(c * LANES, (c + 1) * LANES)
            step = STEP_SIZE * upd_t[(j * panels + c) * blocks : (j * panels + c + 1) * blocks, :]
            new_params[j, :, cols] = (params[j, :, cols].astype(F32) - step).astype(BF16)
    for move in moves:
        move.wait()


def on_device(grads, params, owner_slot, left_stats, right_stats, left_root, right_root):
    blocks, _, rows, width = grads.shape
    nf = lax.axis_size("fsdp")
    nx = lax.axis_size("rep")
    slots, stripe, _ = left_stats.shape
    panels = width // LANES
    half = width // 2
    packet = rows * panels
    groups = 8 if nf >= 64 else 2
    flat = grads.reshape(blocks * packet, 1, LANES)
    params_t = params.reshape(blocks, rows, width).transpose(1, 0, 2)
    hbm = pl.BlockSpec(memory_space=pltpu.HBM)
    vmem = pl.BlockSpec(memory_space=pltpu.VMEM)
    smem = pl.BlockSpec(memory_space=pltpu.SMEM)
    dma = pltpu.SemaphoreType.DMA
    back, scales, left, right = pl.pallas_call(
        functools.partial(kernel, nf, nx, rows, groups, blocks),
        out_shape=(
            pltpu.VMEM((slots, nf, panels, rows, 1, LANES), F32),
            pltpu.VMEM((nf, slots, 1, LANES), F32),
            pltpu.VMEM(left_stats.shape, F32),
            pltpu.VMEM(right_stats.shape, F32),
        ),
        in_specs=[hbm, hbm, hbm, hbm, hbm, hbm],
        out_specs=(vmem, vmem, vmem, vmem),
        scratch_shapes=[
            pltpu.VMEM((1, blocks), jnp.int32),
            pltpu.VMEM((1, slots * nf), jnp.int32),
            pltpu.SMEM((1, slots * nf), jnp.int32),
            pltpu.VMEM(((blocks + 1) * packet, 1, LANES), F32),
            pltpu.VMEM((slots, nf, panels - 1, rows, 1, LANES), F32),
            pltpu.VMEM((nx, (blocks + 1) * rows, 1, LANES), F32),
            pltpu.VMEM((slots, nf, nx, rows, 1, LANES), F32),
            pltpu.VMEM((slots, nx, panels, stripe, 1, LANES), F32),
            pltpu.VMEM((slots, panels, stripe, 1, LANES), F32),
            pltpu.VMEM((slots, stripe, width), F32),
            pltpu.VMEM((slots, stripe, width), F32),
            pltpu.VMEM((slots, stripe, width), F32),
            pltpu.VMEM((slots, 3, half, half), F32),
            pltpu.VMEM((slots, 3, half, half), BF16),
            pltpu.VMEM((slots, 3, half, half), BF16),
            pltpu.VMEM((slots, width, width), BF16),
            pltpu.VMEM((slots, width, width), BF16),
            pltpu.VMEM((2 * LANES, width), F32),
            pltpu.VMEM((slots, nx, stripe, stripe), BF16),
            pltpu.VMEM((slots, nx, stripe, stripe), BF16),
            pltpu.VMEM((2, stripe, half), F32),
            pltpu.VMEM((2, stripe, half), BF16),
            pltpu.VMEM((2, stripe, half), BF16),
            pltpu.VMEM((slots, nx, 8, LANES), F32),
            pltpu.VMEM((slots, 1, LANES), F32),
            dma((10,)),
            dma((slots,)),
            dma((slots, groups)),
            dma((slots, 4)),
            dma((slots, 4)),
            dma((slots, 2, groups)),
            dma((slots, 2, groups)),
            dma((slots, groups)),
            dma((slots, groups)),
            dma((slots, nx - 1)),
            dma((slots, nx - 1)),
            dma((3,)),
            dma((3,)),
            dma(()),
            dma(()),
            dma((4,)),
            dma((4,)),
            dma((slots,)),
            dma((slots,)),
            pltpu.VMEM((2 * LANES, LANES), F32),
        ],
        compiler_params=pltpu.CompilerParams(
            collective_id=0, has_side_effects=True, vmem_limit_bytes=60 * 1024 * 1024
        ),
    )(owner_slot.reshape(1, blocks), flat, left_root, right_root, left_stats, right_stats)
    update, new_params, new_left, new_right = pl.pallas_call(
        finish,
        out_shape=(
            jax.ShapeDtypeStruct((blocks * packet, LANES), F32),
            jax.ShapeDtypeStruct((rows, blocks, width), BF16),
            jax.ShapeDtypeStruct(left_stats.shape, F32),
            jax.ShapeDtypeStruct(right_stats.shape, F32),
        ),
        in_specs=[smem, vmem, vmem, vmem, vmem, vmem],
        out_specs=(vmem, vmem, hbm, hbm),
        scratch_shapes=[
            pltpu.VMEM((blocks * packet, LANES), F32),
            dma((2,)),
        ],
        compiler_params=pltpu.CompilerParams(vmem_limit_bytes=16 * 1024 * 1024),
    )(owner_slot, back.reshape(slots * nf * packet, LANES), scales.reshape(nf * slots, LANES), params_t, left, right)
    update = update.reshape(blocks, 1, rows, width)
    new_params = new_params.transpose(1, 0, 2).reshape(blocks, 1, rows, width)
    return (new_params, update, new_left, new_right)


def solution(mesh):
    in_specs = (
        P(None, "rep", "fsdp", None),
        P(None, "rep", "fsdp", None),
        P(),
        P("fsdp", "rep", None),
        P("fsdp", "rep", None),
        P("fsdp", "rep", None),
        P("fsdp", "rep", None),
    )
    out_specs = (
        P(None, "rep", "fsdp", None),
        P(None, "rep", "fsdp", None),
        P("fsdp", "rep", None),
        P("fsdp", "rep", None),
    )
    return jax.shard_map(
        on_device, mesh=mesh, in_specs=in_specs, out_specs=out_specs, check_vma=False
    )
```

```python
import functools

import jax
import jax.numpy as jnp
from jax import lax
from jax.experimental import pallas as pl
from jax.experimental.pallas import tpu as pltpu
from jax.sharding import PartitionSpec as P

STAT_DECAY = 0.95
STEP_SIZE = 0.25
EPSILON = 1e-06
LANES = 128
VIA_MATE = ((2, 4, 6), (1, 3, 5, 7))
F32 = jnp.float32
BF16 = jnp.bfloat16
NN = (((1,), (0,)), ((), ()))
NT = (((1,), (1,)), ((), ()))


def split(value):
    high = value.astype(BF16)
    return high, (value - high.astype(F32)).astype(BF16)


def dot3(left, right, dims):
    dot = functools.partial(lax.dot_general, dimension_numbers=dims, preferred_element_type=F32)
    return dot(left[0], right[0]) + (dot(left[0], right[1]) + dot(left[1], right[0]))


def kernel(
    nf, nx, rows, groups, blocks,
    owner, grads, left_root, right_root, left_stats, right_stats,
    back, scales, new_left, new_right,
    owner_v, blocks_v, slot_block, grads_v, send, last, send_last, gath, ret, left_v, lstat_v, rstat_v,
    root_f, root_h, root_l, gh, gl, gt, lh, ll, mixed, lgh, lgl, sq, scale_v,
    in_sem, a_send, a_recv, r_send, r_recv, x_send, x_recv, f_send, f_recv,
    s_send, s_recv, u_send, u_recv, c_send, c_recv, q_send, q_recv, p_send, p_recv, turned,
):
    slots, stripe, width = left_v.shape
    panels = width // LANES
    half = width // 2
    packet = rows * panels
    front = panels - 1
    sent = rows * front
    size = nf // groups
    chunk = size * rows
    me = lax.axis_index("fsdp")
    x = lax.axis_index("rep")
    mz, mg = me // size, me % size
    right_x, left_x, far_x = (x + 1) % nx, (x + nx - 1) % nx, (x + 2) % nx
    h, pos = x // 2, x % 2
    mate = h * 2 + 1 - pos
    other = jnp.where(pos == 0, left_x, right_x)

    def at_x(target):
        return {"fsdp": me, "rep": target}

    def at_f(target):
        return {"fsdp": target, "rep": x}

    def remote(src, dst, send_sem, recv_sem, device):
        return pltpu.make_async_remote_copy(
            src_ref=src, dst_ref=dst, send_sem=send_sem, recv_sem=recv_sem,
            device_id=device, device_id_type=pl.DeviceIdType.MESH,
        )

    def await_bytes(ref, sem):
        pltpu.make_async_copy(ref, ref, sem).wait()

    order = [0]
    for step in range(groups // 2, 0, -1):
        order.append(step)
        if step != groups - step:
            order.append(groups - step)

    load_grads = pltpu.make_async_copy(grads, grads_v.at[pl.ds(0, blocks * packet)], in_sem.at[0])
    load_grads.start()
    load_owner = pltpu.make_async_copy(owner, owner_v, in_sem.at[9])
    load_owner.start()
    load_left = pltpu.make_async_copy(left_root, left_v, in_sem.at[1])
    load_left.start()
    loads_r = []
    for t in range(slots):
        for kind in range(2):
            col = h if kind == 0 else 1 - h
            cols = pl.ds(pl.multiple_of(col * half, LANES), half)
            src = right_root.at[t, :, cols]
            load = pltpu.make_async_copy(
                src, root_f.at[t, kind, pl.ds(pl.multiple_of(pos * stripe, 8), stripe)], in_sem.at[2 + 2 * t + kind]
            )
            load.start()
            loads_r.append(load)
    load_ls = pltpu.make_async_copy(left_stats, lstat_v, in_sem.at[6])
    load_ls.start()
    load_rs = pltpu.make_async_copy(right_stats, rstat_v, in_sem.at[7])
    load_rs.start()

    barrier = pltpu.get_barrier_semaphore()

    def greet(k, carry):
        pl.semaphore_signal(barrier, inc=1, device_id=at_f((me + k) % nf), device_id_type=pl.DeviceIdType.MESH)
        return carry

    lax.fori_loop(1, nf, greet, 0)
    for d in range(1, nx):
        pl.semaphore_signal(barrier, inc=1, device_id=at_x((x + d) % nx), device_id_type=pl.DeviceIdType.MESH)

    load_owner.wait()
    row = jnp.broadcast_to(owner_v[...], (blocks, blocks))
    down = lax.broadcasted_iota(jnp.int32, (blocks, blocks), 0)
    along = lax.broadcasted_iota(jnp.int32, (blocks, blocks), 1)
    column = jnp.sum(jnp.where(down == along, row, 0), axis=1, keepdims=True)
    slot_ids = lax.broadcasted_iota(jnp.int32, (blocks, slots * nf), 1)
    block_ids = lax.broadcasted_iota(jnp.int32, (blocks, slots * nf), 0)
    held = blocks + jnp.sum(jnp.where(column == slot_ids, block_ids - blocks, 0), axis=0, keepdims=True)
    blocks_v[...] = jnp.maximum(held, 0)
    to_smem = pltpu.make_async_copy(blocks_v, slot_block, in_sem.at[8])
    to_smem.start()
    load_grads.wait()
    flat_grads = grads_v.reshape((blocks + 1) * packet, LANES)
    flat_grads[pl.ds(blocks * packet, packet), :] = jnp.zeros((packet, LANES), F32)
    flat_last = last.reshape(nx * (blocks + 1) * rows, LANES)
    for i in range(nx):
        flat_last[pl.ds((i * (blocks + 1) + blocks) * rows, rows), :] = jnp.zeros((rows, LANES), F32)
    own_last = flat_grads[pl.ds(front, blocks * rows, stride=panels), :]
    flat_last[pl.ds(x * (blocks + 1) * rows, blocks * rows), :] = own_last
    pl.semaphore_wait(barrier, nf - 1 + nx - 1)

    def diag(t, kind, q):
        return root_f.at[t, kind, pl.ds(pl.multiple_of(q * stripe, 8), stripe), pl.ds(pl.multiple_of(q * LANES, LANES), 2 * LANES)]

    my_rows = pl.ds(pl.multiple_of(pos * stripe, 8), stripe)
    mate_rows = pl.ds(pl.multiple_of((1 - pos) * stripe, 8), stripe)

    def root_copy(t, kind):
        src, dst = (
            (diag(t, 0, pos), diag(t, 0, pos)),
            (root_f.at[t, 1, my_rows], root_f.at[t, 1, my_rows]),
            (root_f.at[t, 0, my_rows], root_f.at[t, 2, my_rows]),
            (diag(t, 0, 1 - pos), diag(t, 2, 1 - pos)),
        )[kind]
        return remote(src, dst, r_send.at[t, kind], r_recv.at[t, kind], at_x(mate if kind < 2 else other))

    def root_arrival(t, kind):
        ref = (
            diag(t, 0, 1 - pos), root_f.at[t, 1, mate_rows], root_f.at[t, 2, mate_rows], diag(t, 2, pos)
        )[kind]
        remote(ref, ref, r_send.at[t, kind], r_recv.at[t, kind], at_x(mate if kind < 2 else other)).wait_recv()

    span = blocks * rows
    low, high = pl.ds(0, span // 2), pl.ds(span // 2, span // 2)

    def last_copy(kind):
        ref = (last.at[x, pl.ds(0, span)], last.at[x, pl.ds(0, span)], last.at[other, low], last.at[mate, high])[kind]
        return remote(ref, ref, q_send.at[kind], q_recv.at[kind], at_x(mate if kind % 2 == 0 else other))

    def last_arrival(kind):
        ref = (last.at[mate, pl.ds(0, span)], last.at[other, pl.ds(0, span)], last.at[far_x, low], last.at[far_x, high])[kind]
        remote(ref, ref, q_send.at[kind], q_recv.at[kind], at_x(mate if kind % 2 == 0 else other)).wait_recv()

    last_copy(0).start()
    last_copy(1).start()
    for t in range(slots):
        loads_r[2 * t].wait()
        loads_r[2 * t + 1].wait()
        root_copy(t, 2).start()
        root_copy(t, 0).start()
        if t == 0:
            root_copy(t, 1).start()

    to_smem.wait()
    flat_send = send.reshape(slots * nf * sent, LANES)
    flat_send_last = send_last.reshape(slots * nf * nx * rows, LANES)

    def pack(t, dest):
        block = slot_block[0, slots * dest + t]
        for j in range(rows):
            value = flat_grads[pl.ds(block * packet + panels * j, front), :]
            flat_send[pl.ds((t * nf + dest) * sent + j, front, stride=rows), :] = value

    def pack_last(t, dest):
        block = slot_block[0, slots * dest + t]
        for i in range(nx):
            value = flat_last[pl.ds((i * (blocks + 1) + block) * rows, rows), :]
            flat_send_last[pl.ds(((t * nf + dest) * nx + i) * rows, rows), :] = value

    def give_rows(t):
        mine = gath.at[t, x, pl.ds(0, front), pl.ds(me * rows, rows)]
        pack(t, me)
        pltpu.make_async_copy(send.at[t, me], mine, a_recv.at[t, mz]).start()
        for offset in order:
            dz = (mz + offset) % groups

            def post(k, carry, dz=dz):
                dest = dz * size + (mg + k) % size
                pack(t, dest)
                remote(send.at[t, dest], mine, a_send.at[t], a_recv.at[t, mz], at_f(dest)).start()
                return carry

            lax.fori_loop(1 if offset == 0 else 0, size, post, 0)

    def give_last(t):
        mine = gath.at[t, :, front, pl.ds(me * rows, rows)]
        pack_last(t, me)
        pltpu.make_async_copy(send_last.at[t, me], mine, p_recv.at[t]).start()
        for offset in order:
            dz = (mz + offset) % groups

            def post(k, carry, dz=dz):
                dest = dz * size + (mg + k) % size
                pack_last(t, dest)
                remote(send_last.at[t, dest], mine, p_send.at[t], p_recv.at[t], at_f(dest)).start()
                return carry

            lax.fori_loop(1 if offset == 0 else 0, size, post, 0)

    def split_left():
        load_left.wait()
        for t in range(slots):
            for i in range(nx):
                lh[t, i], ll[t, i] = split(left_v[t, :, i * stripe : (i + 1) * stripe])


    def rows_of(k):
        source = (mz + groups - order[k]) % groups
        return source, pl.ds(source * chunk, chunk)

    sides = (mate, other)

    def direct(t, k, side):
        source, part = rows_of(k)
        ref = gath.at[t, x, pl.ds(0, front), part]
        return remote(ref, ref, x_send.at[t, side, k], x_recv.at[t, side, k], at_x(sides[side]))

    def arrival(t, k, side):
        source, part = rows_of(k)
        ref = gath.at[t, sides[side], pl.ds(0, front), part]
        return remote(ref, ref, x_send.at[t, side, k], x_recv.at[t, side, k], at_x(sides[side]))

    def forward(t, k):
        source, part = rows_of(k)
        to = 0 if k in VIA_MATE[t] else 1
        ref = gath.at[t, sides[1 - to], pl.ds(0, front), part]
        return remote(ref, ref, f_send.at[t, k], f_recv.at[t, k], at_x(sides[to]))

    def far_arrival(t, k):
        source, part = rows_of(k)
        ref = gath.at[t, far_x, pl.ds(0, front), part]
        return remote(ref, ref, f_send.at[t, k], f_recv.at[t, k], at_x(mate))

    def spread(t):
        for k in range(groups):
            source, part = rows_of(k)
            await_bytes(gath.at[t, x, pl.ds(0, front), part], a_recv.at[t, source])
            direct(t, k, 0).start()
            direct(t, k, 1).start()

    def relay(t):
        for k in range(groups):
            arrival(t, k, 1 if k in VIA_MATE[t] else 0).wait_recv()
            forward(t, k).start()

    def gather_rest(t):
        for k in range(groups):
            arrival(t, k, 0 if k in VIA_MATE[t] else 1).wait_recv()

    g4 = gath.reshape(slots, nx, panels, stripe, LANES)
    ret4 = ret.reshape(slots, panels, stripe, LANES)

    def take(t, i):
        total = jnp.zeros((1, LANES), F32)
        part = pl.ds(pl.multiple_of(i * stripe, 16), stripe)
        for c in range(panels):
            value = g4[t, i, c]
            total = total + jnp.sum(value * value, axis=0, keepdims=True)
            high, low = split(value)
            gh[t, part, c * LANES : (c + 1) * LANES] = high
            gl[t, part, c * LANES : (c + 1) * LANES] = low
        return total

    def mix(t, i, place):
        part = pl.ds(pl.multiple_of(i * stripe, 16), stripe)
        for c in range(2):
            cols = slice(c * half, (c + 1) * half)
            term = dot3((lh[t, i], ll[t, i]), (gh[t, part, cols], gl[t, part, cols]), NN)
            if place == 0:
                mixed[c] = term
            elif place < nx - 1:
                mixed[c] = mixed[c] + term
            else:
                lgh[c], lgl[c] = split(mixed[c] + term)

    per = half // LANES

    def precondition(t, near_part):
        near = (lgh[h], lgl[h])
        away = (lgh[1 - h], lgl[1 - h])
        root = [(root_h[t, kind], root_l[t, kind]) for kind in range(3)]
        if near_part:
            part = dot3(near, root[0], NN) + dot3(away, root[1], NT)
        else:
            part = dot3(near, root[1], NN) + dot3(away, root[2], NN)
        first = (h if near_part else 1 - h) * per
        for c in range(per):
            ret4[t, first + c] = part[:, c * LANES : (c + 1) * LANES]
        return jnp.sum(part * part, axis=0, keepdims=True)

    def square_send(t, squares):
        sq[t, x] = jnp.broadcast_to(jnp.sum(squares, axis=1, keepdims=True), sq.shape[2:])
        for d in range(1, nx):
            remote(sq.at[t, x], sq.at[t, x], s_send.at[t, d - 1], s_recv.at[t, d - 1], at_x((x + d) % nx)).start()

    def scale_of(t, grad_squares):
        for d in range(1, nx):
            ref = sq.at[t, (x + nx - d) % nx]
            remote(ref, ref, s_send.at[t, d - 1], s_recv.at[t, d - 1], at_x((x + d) % nx)).wait_recv()
        prec_mean = (((sq[t, 0] + sq[t, 1]) + sq[t, 2]) + sq[t, 3]) / (width * width)
        grad_mean = jnp.sum(grad_squares, axis=1, keepdims=True) / (width * width)
        scale_v[t] = jnp.sqrt(grad_mean / (prec_mean[0:1, :] + EPSILON))

    def to_all(post):
        for offset in order[1:] + order[:1]:
            dz = (mz + offset) % groups

            def body(k, carry, dz=dz):
                post(dz * size + (mg + k) % size)
                return carry

            lax.fori_loop(1 if offset == 0 else 0, size, body, 0)

    def give_back(t, part, first, count):
        span = pl.ds(first, count)

        def post(dest):
            src = ret.at[t, span, pl.ds(dest * rows, rows)]
            remote(src, back.at[t, me, span], u_send.at[part], u_recv.at[part], at_f(dest)).start()

        own = ret.at[t, span, pl.ds(me * rows, rows)]
        pltpu.make_async_copy(own, back.at[t, me, span], u_recv.at[part]).start()
        to_all(post)

    def give_scales():
        pltpu.make_async_copy(scale_v, scales.at[me], c_recv).start()
        to_all(lambda dest: remote(scale_v, scales.at[me], c_send, c_recv, at_f(dest)).start())

    def left_gram(t):
        mine = pl.ds(pl.multiple_of(x * stripe, 16), stripe)
        ours = (gh[t, mine], gl[t, mine])
        for n in range(3):
            part = slice(n * 256, (n + 1) * 256)
            gram = dot3(ours, (gh[t, part], gl[t, part]), NT)
            new_left[t, :, part] = STAT_DECAY * lstat_v[t, :, part] + (1.0 - STAT_DECAY) * gram

    def right_gram(t):
        first = (3 * x) // 2
        for i in range(nx):
            pair = jnp.concatenate([g4[t, i, first], g4[t, i, first + 1]], axis=1)
            gt[:, i * stripe : (i + 1) * stripe] = pair.T
        ours = split(gt[pl.ds(pl.multiple_of(pos * (LANES // 2), 8), stripe), :])
        for n in range(3):
            part = slice(n * 256, (n + 1) * 256)
            gram = dot3(ours, (gh[t, :, part], gl[t, :, part]), NN)
            new_right[t, :, part] = STAT_DECAY * rstat_v[t, :, part] + (1.0 - STAT_DECAY) * gram

    def mirror(t, kind, q):
        panel = pl.ds(pl.multiple_of((1 - q) * 2 * LANES, LANES), LANES)
        wide = root_f[t, kind, panel, pl.ds(pl.multiple_of(q * LANES, LANES), 2 * LANES)]
        turned[...] = wide.T
        part = turned[pl.ds(pl.multiple_of(q * (LANES // 2), 8), stripe), :]
        root_f[t, kind, pl.ds(pl.multiple_of(q * stripe, 8), stripe), panel] = part

    def take_root(t, kind):
        root_h[t, kind], root_l[t, kind] = split(root_f[t, kind])

    totals = [None] * slots
    give_rows(0)
    for kind in range(2):
        last_arrival(kind)
    for kind in range(2, 4):
        last_copy(kind).start()
    root_arrival(0, 0)
    root_copy(0, 3).start()
    give_rows(1)
    split_left()
    spread(0)
    for kind in range(2, 4):
        last_arrival(kind)
    give_last(0)
    root_arrival(0, 1)
    mirror(0, 0, 1 - pos)
    take_root(0, 0)
    take_root(0, 1)
    relay(0)
    spread(1)
    root_copy(1, 1).start()
    give_last(1)
    root_arrival(0, 2)
    root_arrival(0, 3)
    mirror(0, 2, pos)
    take_root(0, 2)
    await_bytes(gath.at[0, :, front], p_recv.at[0])
    totals[0] = take(0, x)
    mix(0, x, 0)
    gather_rest(0)
    for place, i in ((1, mate), (2, other)):
        totals[0] = totals[0] + take(0, i)
        mix(0, i, place)
    for k in range(groups):
        far_arrival(0, k).wait_recv()
    totals[0] = totals[0] + take(0, far_x)
    mix(0, far_x, 3)
    square_send(0, precondition(0, True) + precondition(0, False))
    give_back(0, 0, 0, panels)
    relay(1)
    root_arrival(1, 0)
    root_copy(1, 3).start()
    root_arrival(1, 1)
    mirror(1, 0, 1 - pos)
    take_root(1, 0)
    take_root(1, 1)
    scale_of(0, totals[0])
    load_ls.wait()
    left_gram(0)
    await_bytes(gath.at[1, :, front], p_recv.at[1])
    totals[1] = take(1, x)
    mix(1, x, 0)
    gather_rest(1)
    for place, i in ((1, mate), (2, other)):
        totals[1] = totals[1] + take(1, i)
        mix(1, i, place)
    for k in range(groups):
        far_arrival(1, k).wait_recv()
    totals[1] = totals[1] + take(1, far_x)
    mix(1, far_x, 3)
    squares = precondition(1, True)
    give_back(1, 1, h * per, per)
    root_arrival(1, 2)
    root_arrival(1, 3)
    mirror(1, 2, pos)
    take_root(1, 2)
    square_send(1, squares + precondition(1, False))
    give_back(1, 2, (1 - h) * per, per)
    scale_of(1, totals[1])
    give_scales()
    load_rs.wait()
    right_gram(0)
    left_gram(1)
    right_gram(1)
    await_bytes(back.at[0], u_recv.at[0])
    await_bytes(back.at[1, :, pl.ds(h * per, per)], u_recv.at[1])
    await_bytes(back.at[1, :, pl.ds((1 - h) * per, per)], u_recv.at[2])
    await_bytes(scales, c_recv)

    for t in range(slots):
        await_bytes(send.at[t, pl.ds(0, nf - 1)], a_send.at[t])
        for k in range(groups):
            direct(t, k, 0).wait_send()
            direct(t, k, 1).wait_send()
            forward(t, k).wait_send()
        for d in range(1, nx):
            remote(sq.at[t, x], sq.at[t, x], s_send.at[t, d - 1], s_recv.at[t, d - 1], at_x((x + d) % nx)).wait_send()
        for kind in range(4):
            root_copy(t, kind).wait_send()
    await_bytes(back.at[0, pl.ds(0, nf - 1)], u_send.at[0])
    await_bytes(back.at[1, pl.ds(0, nf - 1), pl.ds(0, per)], u_send.at[1])
    await_bytes(back.at[1, pl.ds(0, nf - 1), pl.ds(0, per)], u_send.at[2])
    await_bytes(scales.at[pl.ds(0, nf - 1)], c_send)
    for kind in range(4):
        last_copy(kind).wait_send()
    for t in range(slots):
        await_bytes(send_last.at[t, pl.ds(0, nf - 1)], p_send.at[t])


def finish(owner, back, scales, params, left, right, update, new_params, new_left, new_right, upd_t, upd_v, par_v, sem):
    moves = (pltpu.make_async_copy(left, new_left, sem.at[0]), pltpu.make_async_copy(right, new_right, sem.at[1]))
    for move in moves:
        move.start()
    rows, blocks, width = params.shape
    panels = width // LANES
    packet = rows * panels
    slots = left.shape[0]
    nf = back.shape[0] // (packet * slots)

    def place(b, carry):
        slot = owner[b]
        start = ((slot % slots) * nf + slot // slots) * packet
        scale = scales[pl.ds(slot, 1), :]
        for c in range(panels):
            value = back[pl.ds(start + rows * c, rows), :] * scale
            upd_v[pl.ds(b * packet + c, rows, stride=panels), :] = value
            upd_t[pl.ds(c * blocks + b, rows, stride=panels * blocks), :] = value
        return carry

    quarter = blocks // 4
    outs = []
    for q in range(4):
        lax.fori_loop(q * quarter, (q + 1) * quarter, place, 0, unroll=4)
        some = pl.ds(q * quarter * packet, quarter * packet)
        outs.append(pltpu.make_async_copy(upd_v.at[some], update.at[some], sem.at[2 + q]))
        outs[-1].start()
        part = slice(q * quarter, (q + 1) * quarter)
        for j in range(rows):
            for c in range(panels):
                cols = slice(c * LANES, (c + 1) * LANES)
                first = (j * panels + c) * blocks + q * quarter
                step = STEP_SIZE * upd_t[first : first + quarter, :]
                par_v[j, part, cols] = (params[j, part, cols].astype(F32) - step).astype(BF16)
        some = pl.ds(q * quarter, quarter)
        outs.append(pltpu.make_async_copy(par_v.at[:, some], new_params.at[:, some], sem.at[6 + q]))
        outs[-1].start()
    for out in outs:
        out.wait()
    for move in moves:
        move.wait()


def on_device(grads, params, owner_slot, left_stats, right_stats, left_root, right_root):
    blocks, _, rows, width = grads.shape
    nf = lax.axis_size("fsdp")
    nx = lax.axis_size("rep")
    slots, stripe, _ = left_stats.shape
    panels = width // LANES
    half = width // 2
    packet = rows * panels
    groups = 8 if nf >= 64 else 2
    flat = grads.reshape(blocks * packet, 1, LANES)
    params_t = params.reshape(blocks, rows, width).transpose(1, 0, 2)
    hbm = pl.BlockSpec(memory_space=pltpu.HBM)
    vmem = pl.BlockSpec(memory_space=pltpu.VMEM)
    smem = pl.BlockSpec(memory_space=pltpu.SMEM)
    dma = pltpu.SemaphoreType.DMA
    back, scales, left, right = pl.pallas_call(
        functools.partial(kernel, nf, nx, rows, groups, blocks),
        out_shape=(
            pltpu.VMEM((slots, nf, panels, rows, 1, LANES), F32),
            pltpu.VMEM((nf, slots, 1, LANES), F32),
            pltpu.VMEM(left_stats.shape, F32),
            pltpu.VMEM(right_stats.shape, F32),
        ),
        in_specs=[hbm, hbm, hbm, hbm, hbm, hbm],
        out_specs=(vmem, vmem, vmem, vmem),
        scratch_shapes=[
            pltpu.VMEM((1, blocks), jnp.int32),
            pltpu.VMEM((1, slots * nf), jnp.int32),
            pltpu.SMEM((1, slots * nf), jnp.int32),
            pltpu.VMEM(((blocks + 1) * packet, 1, LANES), F32),
            pltpu.VMEM((slots, nf, panels - 1, rows, 1, LANES), F32),
            pltpu.VMEM((nx, (blocks + 1) * rows, 1, LANES), F32),
            pltpu.VMEM((slots, nf, nx, rows, 1, LANES), F32),
            pltpu.VMEM((slots, nx, panels, stripe, 1, LANES), F32),
            pltpu.VMEM((slots, panels, stripe, 1, LANES), F32),
            pltpu.VMEM((slots, stripe, width), F32),
            pltpu.VMEM((slots, stripe, width), F32),
            pltpu.VMEM((slots, stripe, width), F32),
            pltpu.VMEM((slots, 3, half, half), F32),
            pltpu.VMEM((slots, 3, half, half), BF16),
            pltpu.VMEM((slots, 3, half, half), BF16),
            pltpu.VMEM((slots, width, width), BF16),
            pltpu.VMEM((slots, width, width), BF16),
            pltpu.VMEM((2 * LANES, width), F32),
            pltpu.VMEM((slots, nx, stripe, stripe), BF16),
            pltpu.VMEM((slots, nx, stripe, stripe), BF16),
            pltpu.VMEM((2, stripe, half), F32),
            pltpu.VMEM((2, stripe, half), BF16),
            pltpu.VMEM((2, stripe, half), BF16),
            pltpu.VMEM((slots, nx, 8, LANES), F32),
            pltpu.VMEM((slots, 1, LANES), F32),
            dma((10,)),
            dma((slots,)),
            dma((slots, groups)),
            dma((slots, 4)),
            dma((slots, 4)),
            dma((slots, 2, groups)),
            dma((slots, 2, groups)),
            dma((slots, groups)),
            dma((slots, groups)),
            dma((slots, nx - 1)),
            dma((slots, nx - 1)),
            dma((3,)),
            dma((3,)),
            dma(()),
            dma(()),
            dma((4,)),
            dma((4,)),
            dma((slots,)),
            dma((slots,)),
            pltpu.VMEM((2 * LANES, LANES), F32),
        ],
        compiler_params=pltpu.CompilerParams(
            collective_id=0, has_side_effects=True, vmem_limit_bytes=60 * 1024 * 1024
        ),
    )(owner_slot.reshape(1, blocks), flat, left_root, right_root, left_stats, right_stats)
    update, new_params, new_left, new_right = pl.pallas_call(
        finish,
        out_shape=(
            jax.ShapeDtypeStruct((blocks * packet, LANES), F32),
            jax.ShapeDtypeStruct((rows, blocks, width), BF16),
            jax.ShapeDtypeStruct(left_stats.shape, F32),
            jax.ShapeDtypeStruct(right_stats.shape, F32),
        ),
        in_specs=[smem, vmem, vmem, vmem, vmem, vmem],
        out_specs=(hbm, hbm, hbm, hbm),
        scratch_shapes=[
            pltpu.VMEM((blocks * packet, LANES), F32),
            pltpu.VMEM((blocks * packet, LANES), F32),
            pltpu.VMEM((rows, blocks, width), BF16),
            dma((10,)),
        ],
        compiler_params=pltpu.CompilerParams(vmem_limit_bytes=16 * 1024 * 1024),
    )(owner_slot, back.reshape(slots * nf * packet, LANES), scales.reshape(nf * slots, LANES), params_t, left, right)
    update = update.reshape(blocks, 1, rows, width)
    new_params = new_params.transpose(1, 0, 2).reshape(blocks, 1, rows, width)
    return (new_params, update, new_left, new_right)


def solution(mesh):
    in_specs = (
        P(None, "rep", "fsdp", None),
        P(None, "rep", "fsdp", None),
        P(),
        P("fsdp", "rep", None),
        P("fsdp", "rep", None),
        P("fsdp", "rep", None),
        P("fsdp", "rep", None),
    )
    out_specs = (
        P(None, "rep", "fsdp", None),
        P(None, "rep", "fsdp", None),
        P("fsdp", "rep", None),
        P("fsdp", "rep", None),
    )
    return jax.shard_map(
        on_device, mesh=mesh, in_specs=in_specs, out_specs=out_specs, check_vma=False
    )
```

```python
import functools

import jax
import jax.numpy as jnp
from jax import lax
from jax.experimental import pallas as pl
from jax.experimental.pallas import tpu as pltpu
from jax.sharding import PartitionSpec as P

STAT_DECAY = 0.95
STEP_SIZE = 0.25
EPSILON = 1e-06
LANES = 128
VIA_MATE = ((2, 4, 6), (1, 3, 5, 7))
F32 = jnp.float32
BF16 = jnp.bfloat16
NN = (((1,), (0,)), ((), ()))
NT = (((1,), (1,)), ((), ()))


def split(value):
    high = value.astype(BF16)
    return high, (value - high.astype(F32)).astype(BF16)


def dot3(left, right, dims):
    dot = functools.partial(lax.dot_general, dimension_numbers=dims, preferred_element_type=F32)
    return dot(left[0], right[0]) + (dot(left[0], right[1]) + dot(left[1], right[0]))


def kernel(
    nf, nx, rows, groups, blocks,
    owner, grads, left_root, right_root, left_stats, right_stats,
    back, scales, new_left, new_right,
    owner_v, blocks_v, slot_block, grads_v, send, last, send_last, gath, ret, left_v, lstat_v, rstat_v,
    root_f, root_h, root_l, gh, gl, gt, lh, ll, mixed, lgh, lgl, sq, scale_v,
    in_sem, a_send, a_recv, r_send, r_recv, x_send, x_recv, f_send, f_recv,
    s_send, s_recv, u_send, u_recv, c_send, c_recv, q_send, q_recv, p_send, p_recv, turned,
):
    slots, stripe, width = left_v.shape
    panels = width // LANES
    half = width // 2
    packet = rows * panels
    front = panels - 1
    sent = rows * front
    size = nf // groups
    chunk = size * rows
    me = lax.axis_index("fsdp")
    x = lax.axis_index("rep")
    mz, mg = me // size, me % size
    right_x, left_x, far_x = (x + 1) % nx, (x + nx - 1) % nx, (x + 2) % nx
    h, pos = x // 2, x % 2
    mate = h * 2 + 1 - pos
    other = jnp.where(pos == 0, left_x, right_x)

    def at_x(target):
        return {"fsdp": me, "rep": target}

    def at_f(target):
        return {"fsdp": target, "rep": x}

    def remote(src, dst, send_sem, recv_sem, device):
        return pltpu.make_async_remote_copy(
            src_ref=src, dst_ref=dst, send_sem=send_sem, recv_sem=recv_sem,
            device_id=device, device_id_type=pl.DeviceIdType.MESH,
        )

    def await_bytes(ref, sem):
        pltpu.make_async_copy(ref, ref, sem).wait()

    order = [0]
    for step in range(groups // 2, 0, -1):
        order.append(step)
        if step != groups - step:
            order.append(groups - step)

    load_grads = pltpu.make_async_copy(grads, grads_v.at[pl.ds(0, blocks * packet)], in_sem.at[0])
    load_grads.start()
    load_owner = pltpu.make_async_copy(owner, owner_v, in_sem.at[9])
    load_owner.start()
    loads_r = []
    for t in range(slots):
        for kind in range(2):
            col = h if kind == 0 else 1 - h
            cols = pl.ds(pl.multiple_of(col * half, LANES), half)
            src = right_root.at[t, :, cols]
            load = pltpu.make_async_copy(
                src, root_f.at[t, kind, pl.ds(pl.multiple_of(pos * stripe, 8), stripe)], in_sem.at[2 + 2 * t + kind]
            )
            load.start()
            loads_r.append(load)

    barrier = pltpu.get_barrier_semaphore()

    def greet(k, carry):
        pl.semaphore_signal(barrier, inc=1, device_id=at_f((me + k) % nf), device_id_type=pl.DeviceIdType.MESH)
        return carry

    lax.fori_loop(1, nf, greet, 0)
    for d in range(1, nx):
        pl.semaphore_signal(barrier, inc=1, device_id=at_x((x + d) % nx), device_id_type=pl.DeviceIdType.MESH)

    load_owner.wait()
    row = jnp.broadcast_to(owner_v[...], (blocks, blocks))
    down = lax.broadcasted_iota(jnp.int32, (blocks, blocks), 0)
    along = lax.broadcasted_iota(jnp.int32, (blocks, blocks), 1)
    column = jnp.sum(jnp.where(down == along, row, 0), axis=1, keepdims=True)
    slot_ids = lax.broadcasted_iota(jnp.int32, (blocks, slots * nf), 1)
    block_ids = lax.broadcasted_iota(jnp.int32, (blocks, slots * nf), 0)
    held = blocks + jnp.sum(jnp.where(column == slot_ids, block_ids - blocks, 0), axis=0, keepdims=True)
    blocks_v[...] = jnp.maximum(held, 0)
    to_smem = pltpu.make_async_copy(blocks_v, slot_block, in_sem.at[8])
    to_smem.start()
    load_grads.wait()
    flat_grads = grads_v.reshape((blocks + 1) * packet, LANES)
    flat_grads[pl.ds(blocks * packet, packet), :] = jnp.zeros((packet, LANES), F32)
    flat_last = last.reshape(nx * (blocks + 1) * rows, LANES)
    for i in range(nx):
        flat_last[pl.ds((i * (blocks + 1) + blocks) * rows, rows), :] = jnp.zeros((rows, LANES), F32)
    own_last = flat_grads[pl.ds(front, blocks * rows, stride=panels), :]
    flat_last[pl.ds(x * (blocks + 1) * rows, blocks * rows), :] = own_last
    pl.semaphore_wait(barrier, nf - 1 + nx - 1)

    def diag(t, kind, q):
        return root_f.at[t, kind, pl.ds(pl.multiple_of(q * stripe, 8), stripe), pl.ds(pl.multiple_of(q * LANES, LANES), 2 * LANES)]

    my_rows = pl.ds(pl.multiple_of(pos * stripe, 8), stripe)
    mate_rows = pl.ds(pl.multiple_of((1 - pos) * stripe, 8), stripe)

    def root_copy(t, kind):
        src, dst = (
            (diag(t, 0, pos), diag(t, 0, pos)),
            (root_f.at[t, 1, my_rows], root_f.at[t, 1, my_rows]),
            (root_f.at[t, 0, my_rows], root_f.at[t, 2, my_rows]),
            (diag(t, 0, 1 - pos), diag(t, 2, 1 - pos)),
        )[kind]
        return remote(src, dst, r_send.at[t, kind], r_recv.at[t, kind], at_x(mate if kind < 2 else other))

    def root_arrival(t, kind):
        ref = (
            diag(t, 0, 1 - pos), root_f.at[t, 1, mate_rows], root_f.at[t, 2, mate_rows], diag(t, 2, pos)
        )[kind]
        remote(ref, ref, r_send.at[t, kind], r_recv.at[t, kind], at_x(mate if kind < 2 else other)).wait_recv()

    span = blocks * rows
    low, high = pl.ds(0, span // 2), pl.ds(span // 2, span // 2)

    def last_copy(kind):
        ref = (last.at[x, pl.ds(0, span)], last.at[x, pl.ds(0, span)], last.at[other, low], last.at[mate, high])[kind]
        return remote(ref, ref, q_send.at[kind], q_recv.at[kind], at_x(mate if kind % 2 == 0 else other))

    def last_arrival(kind):
        ref = (last.at[mate, pl.ds(0, span)], last.at[other, pl.ds(0, span)], last.at[far_x, low], last.at[far_x, high])[kind]
        remote(ref, ref, q_send.at[kind], q_recv.at[kind], at_x(mate if kind % 2 == 0 else other)).wait_recv()

    last_copy(0).start()
    last_copy(1).start()
    for t in range(slots):
        loads_r[2 * t].wait()
        loads_r[2 * t + 1].wait()
        root_copy(t, 2).start()
        root_copy(t, 0).start()
        if t == 0:
            root_copy(t, 1).start()

    load_left = pltpu.make_async_copy(left_root, left_v, in_sem.at[1])
    load_left.start()
    load_ls = pltpu.make_async_copy(left_stats, lstat_v, in_sem.at[6])
    load_ls.start()
    load_rs = pltpu.make_async_copy(right_stats, rstat_v, in_sem.at[7])
    load_rs.start()

    to_smem.wait()
    flat_send = send.reshape(slots * nf * sent, LANES)
    flat_send_last = send_last.reshape(slots * nf * nx * rows, LANES)

    def pack(t, dest):
        block = slot_block[0, slots * dest + t]
        for j in range(rows):
            value = flat_grads[pl.ds(block * packet + panels * j, front), :]
            flat_send[pl.ds((t * nf + dest) * sent + j, front, stride=rows), :] = value

    def pack_last(t, dest):
        block = slot_block[0, slots * dest + t]
        for i in range(nx):
            value = flat_last[pl.ds((i * (blocks + 1) + block) * rows, rows), :]
            flat_send_last[pl.ds(((t * nf + dest) * nx + i) * rows, rows), :] = value

    def give_rows(t):
        mine = gath.at[t, x, pl.ds(0, front), pl.ds(me * rows, rows)]
        pack(t, me)
        pltpu.make_async_copy(send.at[t, me], mine, a_recv.at[t, mz]).start()
        for offset in order:
            dz = (mz + offset) % groups

            def post(k, carry, dz=dz):
                dest = dz * size + (mg + k) % size
                pack(t, dest)
                remote(send.at[t, dest], mine, a_send.at[t], a_recv.at[t, mz], at_f(dest)).start()
                return carry

            lax.fori_loop(1 if offset == 0 else 0, size, post, 0)

    def give_last(t):
        mine = gath.at[t, :, front, pl.ds(me * rows, rows)]
        pack_last(t, me)
        pltpu.make_async_copy(send_last.at[t, me], mine, p_recv.at[t]).start()
        for offset in order:
            dz = (mz + offset) % groups

            def post(k, carry, dz=dz):
                dest = dz * size + (mg + k) % size
                pack_last(t, dest)
                remote(send_last.at[t, dest], mine, p_send.at[t], p_recv.at[t], at_f(dest)).start()
                return carry

            lax.fori_loop(1 if offset == 0 else 0, size, post, 0)

    def split_left():
        load_left.wait()
        for t in range(slots):
            for i in range(nx):
                lh[t, i], ll[t, i] = split(left_v[t, :, i * stripe : (i + 1) * stripe])


    def rows_of(k):
        source = (mz + groups - order[k]) % groups
        return source, pl.ds(source * chunk, chunk)

    sides = (mate, other)

    def direct(t, k, side):
        source, part = rows_of(k)
        ref = gath.at[t, x, pl.ds(0, front), part]
        return remote(ref, ref, x_send.at[t, side, k], x_recv.at[t, side, k], at_x(sides[side]))

    def arrival(t, k, side):
        source, part = rows_of(k)
        ref = gath.at[t, sides[side], pl.ds(0, front), part]
        return remote(ref, ref, x_send.at[t, side, k], x_recv.at[t, side, k], at_x(sides[side]))

    def forward(t, k):
        source, part = rows_of(k)
        to = 0 if k in VIA_MATE[t] else 1
        ref = gath.at[t, sides[1 - to], pl.ds(0, front), part]
        return remote(ref, ref, f_send.at[t, k], f_recv.at[t, k], at_x(sides[to]))

    def far_arrival(t, k):
        source, part = rows_of(k)
        ref = gath.at[t, far_x, pl.ds(0, front), part]
        return remote(ref, ref, f_send.at[t, k], f_recv.at[t, k], at_x(mate))

    def spread(t):
        for k in range(groups):
            source, part = rows_of(k)
            await_bytes(gath.at[t, x, pl.ds(0, front), part], a_recv.at[t, source])
            direct(t, k, 0).start()
            direct(t, k, 1).start()

    def relay(t):
        for k in range(groups):
            arrival(t, k, 1 if k in VIA_MATE[t] else 0).wait_recv()
            forward(t, k).start()

    def gather_rest(t):
        for k in range(groups):
            arrival(t, k, 0 if k in VIA_MATE[t] else 1).wait_recv()

    g4 = gath.reshape(slots, nx, panels, stripe, LANES)
    ret4 = ret.reshape(slots, panels, stripe, LANES)

    def take(t, i):
        total = jnp.zeros((1, LANES), F32)
        part = pl.ds(pl.multiple_of(i * stripe, 16), stripe)
        for c in range(panels):
            value = g4[t, i, c]
            total = total + jnp.sum(value * value, axis=0, keepdims=True)
            high, low = split(value)
            gh[t, part, c * LANES : (c + 1) * LANES] = high
            gl[t, part, c * LANES : (c + 1) * LANES] = low
        return total

    def mix(t, i, place):
        part = pl.ds(pl.multiple_of(i * stripe, 16), stripe)
        for c in range(2):
            cols = slice(c * half, (c + 1) * half)
            term = dot3((lh[t, i], ll[t, i]), (gh[t, part, cols], gl[t, part, cols]), NN)
            if place == 0:
                mixed[c] = term
            elif place < nx - 1:
                mixed[c] = mixed[c] + term
            else:
                lgh[c], lgl[c] = split(mixed[c] + term)

    per = half // LANES

    def precondition(t, near_part):
        near = (lgh[h], lgl[h])
        away = (lgh[1 - h], lgl[1 - h])
        root = [(root_h[t, kind], root_l[t, kind]) for kind in range(3)]
        if near_part:
            part = dot3(near, root[0], NN) + dot3(away, root[1], NT)
        else:
            part = dot3(near, root[1], NN) + dot3(away, root[2], NN)
        first = (h if near_part else 1 - h) * per
        for c in range(per):
            ret4[t, first + c] = part[:, c * LANES : (c + 1) * LANES]
        return jnp.sum(part * part, axis=0, keepdims=True)

    def square_send(t, squares):
        sq[t, x] = jnp.broadcast_to(jnp.sum(squares, axis=1, keepdims=True), sq.shape[2:])
        for d in range(1, nx):
            remote(sq.at[t, x], sq.at[t, x], s_send.at[t, d - 1], s_recv.at[t, d - 1], at_x((x + d) % nx)).start()

    def scale_of(t, grad_squares):
        for d in range(1, nx):
            ref = sq.at[t, (x + nx - d) % nx]
            remote(ref, ref, s_send.at[t, d - 1], s_recv.at[t, d - 1], at_x((x + d) % nx)).wait_recv()
        prec_mean = (((sq[t, 0] + sq[t, 1]) + sq[t, 2]) + sq[t, 3]) / (width * width)
        grad_mean = jnp.sum(grad_squares, axis=1, keepdims=True) / (width * width)
        scale_v[t] = jnp.sqrt(grad_mean / (prec_mean[0:1, :] + EPSILON))

    def to_all(post):
        for offset in order[1:] + order[:1]:
            dz = (mz + offset) % groups

            def body(k, carry, dz=dz):
                post(dz * size + (mg + k) % size)
                return carry

            lax.fori_loop(1 if offset == 0 else 0, size, body, 0)

    def give_back(t, part, first, count):
        span = pl.ds(first, count)

        def post(dest):
            src = ret.at[t, span, pl.ds(dest * rows, rows)]
            remote(src, back.at[t, me, span], u_send.at[part], u_recv.at[part], at_f(dest)).start()

        own = ret.at[t, span, pl.ds(me * rows, rows)]
        pltpu.make_async_copy(own, back.at[t, me, span], u_recv.at[part]).start()
        to_all(post)

    def give_scales():
        pltpu.make_async_copy(scale_v, scales.at[me], c_recv).start()
        to_all(lambda dest: remote(scale_v, scales.at[me], c_send, c_recv, at_f(dest)).start())

    def left_gram(t):
        mine = pl.ds(pl.multiple_of(x * stripe, 16), stripe)
        ours = (gh[t, mine], gl[t, mine])
        for n in range(3):
            part = slice(n * 256, (n + 1) * 256)
            gram = dot3(ours, (gh[t, part], gl[t, part]), NT)
            new_left[t, :, part] = STAT_DECAY * lstat_v[t, :, part] + (1.0 - STAT_DECAY) * gram

    def right_gram(t):
        first = (3 * x) // 2
        for i in range(nx):
            pair = jnp.concatenate([g4[t, i, first], g4[t, i, first + 1]], axis=1)
            gt[:, i * stripe : (i + 1) * stripe] = pair.T
        ours = split(gt[pl.ds(pl.multiple_of(pos * (LANES // 2), 8), stripe), :])
        for n in range(3):
            part = slice(n * 256, (n + 1) * 256)
            gram = dot3(ours, (gh[t, :, part], gl[t, :, part]), NN)
            new_right[t, :, part] = STAT_DECAY * rstat_v[t, :, part] + (1.0 - STAT_DECAY) * gram

    def mirror(t, kind, q):
        panel = pl.ds(pl.multiple_of((1 - q) * 2 * LANES, LANES), LANES)
        wide = root_f[t, kind, panel, pl.ds(pl.multiple_of(q * LANES, LANES), 2 * LANES)]
        turned[...] = wide.T
        part = turned[pl.ds(pl.multiple_of(q * (LANES // 2), 8), stripe), :]
        root_f[t, kind, pl.ds(pl.multiple_of(q * stripe, 8), stripe), panel] = part

    def take_root(t, kind):
        root_h[t, kind], root_l[t, kind] = split(root_f[t, kind])

    totals = [None] * slots
    give_rows(0)
    for kind in range(2):
        last_arrival(kind)
    for kind in range(2, 4):
        last_copy(kind).start()
    root_arrival(0, 0)
    root_copy(0, 3).start()
    give_rows(1)
    split_left()
    spread(0)
    for kind in range(2, 4):
        last_arrival(kind)
    give_last(0)
    root_arrival(0, 1)
    mirror(0, 0, 1 - pos)
    take_root(0, 0)
    take_root(0, 1)
    relay(0)
    spread(1)
    root_copy(1, 1).start()
    give_last(1)
    root_arrival(0, 2)
    root_arrival(0, 3)
    mirror(0, 2, pos)
    take_root(0, 2)
    await_bytes(gath.at[0, :, front], p_recv.at[0])
    totals[0] = take(0, x)
    mix(0, x, 0)
    gather_rest(0)
    for place, i in ((1, mate), (2, other)):
        totals[0] = totals[0] + take(0, i)
        mix(0, i, place)
    for k in range(groups):
        far_arrival(0, k).wait_recv()
    totals[0] = totals[0] + take(0, far_x)
    mix(0, far_x, 3)
    square_send(0, precondition(0, True) + precondition(0, False))
    give_back(0, 0, 0, panels)
    relay(1)
    root_arrival(1, 0)
    root_copy(1, 3).start()
    root_arrival(1, 1)
    mirror(1, 0, 1 - pos)
    take_root(1, 0)
    take_root(1, 1)
    scale_of(0, totals[0])
    load_ls.wait()
    left_gram(0)
    await_bytes(gath.at[1, :, front], p_recv.at[1])
    totals[1] = take(1, x)
    mix(1, x, 0)
    gather_rest(1)
    for place, i in ((1, mate), (2, other)):
        totals[1] = totals[1] + take(1, i)
        mix(1, i, place)
    for k in range(groups):
        far_arrival(1, k).wait_recv()
    totals[1] = totals[1] + take(1, far_x)
    mix(1, far_x, 3)
    squares = precondition(1, True)
    give_back(1, 1, h * per, per)
    root_arrival(1, 2)
    root_arrival(1, 3)
    mirror(1, 2, pos)
    take_root(1, 2)
    square_send(1, squares + precondition(1, False))
    give_back(1, 2, (1 - h) * per, per)
    scale_of(1, totals[1])
    give_scales()
    load_rs.wait()
    right_gram(0)
    left_gram(1)
    right_gram(1)
    await_bytes(back.at[0], u_recv.at[0])
    await_bytes(back.at[1, :, pl.ds(h * per, per)], u_recv.at[1])
    await_bytes(back.at[1, :, pl.ds((1 - h) * per, per)], u_recv.at[2])
    await_bytes(scales, c_recv)

    for t in range(slots):
        await_bytes(send.at[t, pl.ds(0, nf - 1)], a_send.at[t])
        for k in range(groups):
            direct(t, k, 0).wait_send()
            direct(t, k, 1).wait_send()
            forward(t, k).wait_send()
        for d in range(1, nx):
            remote(sq.at[t, x], sq.at[t, x], s_send.at[t, d - 1], s_recv.at[t, d - 1], at_x((x + d) % nx)).wait_send()
        for kind in range(4):
            root_copy(t, kind).wait_send()
    await_bytes(back.at[0, pl.ds(0, nf - 1)], u_send.at[0])
    await_bytes(back.at[1, pl.ds(0, nf - 1), pl.ds(0, per)], u_send.at[1])
    await_bytes(back.at[1, pl.ds(0, nf - 1), pl.ds(0, per)], u_send.at[2])
    await_bytes(scales.at[pl.ds(0, nf - 1)], c_send)
    for kind in range(4):
        last_copy(kind).wait_send()
    for t in range(slots):
        await_bytes(send_last.at[t, pl.ds(0, nf - 1)], p_send.at[t])


def finish(owner, back, scales, params, left, right, update, new_params, new_left, new_right, upd_t, upd_v, par_v, sem):
    moves = (pltpu.make_async_copy(left, new_left, sem.at[0]), pltpu.make_async_copy(right, new_right, sem.at[1]))
    for move in moves:
        move.start()
    rows, blocks, width = params.shape
    panels = width // LANES
    packet = rows * panels
    slots = left.shape[0]
    nf = back.shape[0] // (packet * slots)

    def place(b, carry):
        slot = owner[b]
        start = ((slot % slots) * nf + slot // slots) * packet
        scale = scales[pl.ds(slot, 1), :]
        for c in range(panels):
            value = back[pl.ds(start + rows * c, rows), :] * scale
            upd_v[pl.ds(b * packet + c, rows, stride=panels), :] = value
            upd_t[pl.ds(c * blocks + b, rows, stride=panels * blocks), :] = value
        return carry

    quarter = blocks // 4
    outs = []
    for q in range(4):
        lax.fori_loop(q * quarter, (q + 1) * quarter, place, 0, unroll=4)
        some = pl.ds(q * quarter * packet, quarter * packet)
        outs.append(pltpu.make_async_copy(upd_v.at[some], update.at[some], sem.at[2 + q]))
        outs[-1].start()
        part = slice(q * quarter, (q + 1) * quarter)
        for j in range(rows):
            for c in range(panels):
                cols = slice(c * LANES, (c + 1) * LANES)
                first = (j * panels + c) * blocks + q * quarter
                step = STEP_SIZE * upd_t[first : first + quarter, :]
                par_v[j, part, cols] = (params[j, part, cols].astype(F32) - step).astype(BF16)
        some = pl.ds(q * quarter, quarter)
        outs.append(pltpu.make_async_copy(par_v.at[:, some], new_params.at[:, some], sem.at[6 + q]))
        outs[-1].start()
    for out in outs:
        out.wait()
    for move in moves:
        move.wait()


def on_device(grads, params, owner_slot, left_stats, right_stats, left_root, right_root):
    blocks, _, rows, width = grads.shape
    nf = lax.axis_size("fsdp")
    nx = lax.axis_size("rep")
    slots, stripe, _ = left_stats.shape
    panels = width // LANES
    half = width // 2
    packet = rows * panels
    groups = 8 if nf >= 64 else 2
    flat = grads.reshape(blocks * packet, 1, LANES)
    params_t = params.reshape(blocks, rows, width).transpose(1, 0, 2)
    hbm = pl.BlockSpec(memory_space=pltpu.HBM)
    vmem = pl.BlockSpec(memory_space=pltpu.VMEM)
    smem = pl.BlockSpec(memory_space=pltpu.SMEM)
    dma = pltpu.SemaphoreType.DMA
    back, scales, left, right = pl.pallas_call(
        functools.partial(kernel, nf, nx, rows, groups, blocks),
        out_shape=(
            pltpu.VMEM((slots, nf, panels, rows, 1, LANES), F32),
            pltpu.VMEM((nf, slots, 1, LANES), F32),
            pltpu.VMEM(left_stats.shape, F32),
            pltpu.VMEM(right_stats.shape, F32),
        ),
        in_specs=[hbm, hbm, hbm, hbm, hbm, hbm],
        out_specs=(vmem, vmem, vmem, vmem),
        scratch_shapes=[
            pltpu.VMEM((1, blocks), jnp.int32),
            pltpu.VMEM((1, slots * nf), jnp.int32),
            pltpu.SMEM((1, slots * nf), jnp.int32),
            pltpu.VMEM(((blocks + 1) * packet, 1, LANES), F32),
            pltpu.VMEM((slots, nf, panels - 1, rows, 1, LANES), F32),
            pltpu.VMEM((nx, (blocks + 1) * rows, 1, LANES), F32),
            pltpu.VMEM((slots, nf, nx, rows, 1, LANES), F32),
            pltpu.VMEM((slots, nx, panels, stripe, 1, LANES), F32),
            pltpu.VMEM((slots, panels, stripe, 1, LANES), F32),
            pltpu.VMEM((slots, stripe, width), F32),
            pltpu.VMEM((slots, stripe, width), F32),
            pltpu.VMEM((slots, stripe, width), F32),
            pltpu.VMEM((slots, 3, half, half), F32),
            pltpu.VMEM((slots, 3, half, half), BF16),
            pltpu.VMEM((slots, 3, half, half), BF16),
            pltpu.VMEM((slots, width, width), BF16),
            pltpu.VMEM((slots, width, width), BF16),
            pltpu.VMEM((2 * LANES, width), F32),
            pltpu.VMEM((slots, nx, stripe, stripe), BF16),
            pltpu.VMEM((slots, nx, stripe, stripe), BF16),
            pltpu.VMEM((2, stripe, half), F32),
            pltpu.VMEM((2, stripe, half), BF16),
            pltpu.VMEM((2, stripe, half), BF16),
            pltpu.VMEM((slots, nx, 8, LANES), F32),
            pltpu.VMEM((slots, 1, LANES), F32),
            dma((10,)),
            dma((slots,)),
            dma((slots, groups)),
            dma((slots, 4)),
            dma((slots, 4)),
            dma((slots, 2, groups)),
            dma((slots, 2, groups)),
            dma((slots, groups)),
            dma((slots, groups)),
            dma((slots, nx - 1)),
            dma((slots, nx - 1)),
            dma((3,)),
            dma((3,)),
            dma(()),
            dma(()),
            dma((4,)),
            dma((4,)),
            dma((slots,)),
            dma((slots,)),
            pltpu.VMEM((2 * LANES, LANES), F32),
        ],
        compiler_params=pltpu.CompilerParams(
            collective_id=0, has_side_effects=True, vmem_limit_bytes=60 * 1024 * 1024
        ),
    )(owner_slot.reshape(1, blocks), flat, left_root, right_root, left_stats, right_stats)
    update, new_params, new_left, new_right = pl.pallas_call(
        finish,
        out_shape=(
            jax.ShapeDtypeStruct((blocks * packet, LANES), F32),
            jax.ShapeDtypeStruct((rows, blocks, width), BF16),
            jax.ShapeDtypeStruct(left_stats.shape, F32),
            jax.ShapeDtypeStruct(right_stats.shape, F32),
        ),
        in_specs=[smem, vmem, vmem, vmem, vmem, vmem],
        out_specs=(hbm, hbm, hbm, hbm),
        scratch_shapes=[
            pltpu.VMEM((blocks * packet, LANES), F32),
            pltpu.VMEM((blocks * packet, LANES), F32),
            pltpu.VMEM((rows, blocks, width), BF16),
            dma((10,)),
        ],
        compiler_params=pltpu.CompilerParams(vmem_limit_bytes=16 * 1024 * 1024),
    )(owner_slot, back.reshape(slots * nf * packet, LANES), scales.reshape(nf * slots, LANES), params_t, left, right)
    update = update.reshape(blocks, 1, rows, width)
    new_params = new_params.transpose(1, 0, 2).reshape(blocks, 1, rows, width)
    return (new_params, update, new_left, new_right)


def solution(mesh):
    in_specs = (
        P(None, "rep", "fsdp", None),
        P(None, "rep", "fsdp", None),
        P(),
        P("fsdp", "rep", None),
        P("fsdp", "rep", None),
        P("fsdp", "rep", None),
        P("fsdp", "rep", None),
    )
    out_specs = (
        P(None, "rep", "fsdp", None),
        P(None, "rep", "fsdp", None),
        P("fsdp", "rep", None),
        P("fsdp", "rep", None),
    )
    return jax.shard_map(
        on_device, mesh=mesh, in_specs=in_specs, out_specs=out_specs, check_vma=False
    )
```
